256 devices in a mesh: shard: 64 (over z, x, core), clus: 4 (over y).
Axes of the slice: x: 4, y: 4, z: 8, core: 2. Of those that a mesh axis runs over, the one named last changes fastest.
Arguments:
- embeddings: bfloat16 [131072, 1024], P(('shard', 'clus')), may hold values from -600 to 600
- cluster: int32 [131072], P(('shard', 'clus')), may hold values from 0 to 255, as said below
- arrival: int32 [131072], P(('shard', 'clus')), may hold values from 0 to 131071, each once
Outputs:
- best_seen: float32 [131072], P(('shard', 'clus'))
The draws below stay inside these ranges and needn't reach their ends.
Inputs may be any that keep to these rules, and one draw needn't show every extreme that they name: Among the 512 rows of one device at most 16 have cluster ids with the same remainder modulo 64; on every device some remainders reach 16.
All inputs are finite; a program needn't handle non-finite values.
Results may differ from the reference program's by a relative error of at most 0.0003.
Values may be sent and summed in bfloat16 or wider, within the bound.
No kernel may reach another device: no remote copies, remote signals or barrier semaphores. Data moves between devices by JAX's collectives and lax.ppermute only.
A program may use at most 64 MiB of HBM per device.

```python
import math
import jax
import jax.numpy as jnp
from jax import lax

D = 1024
ROWS_DEV = 512
CPO = 4
OWNERS = 64
CLUSTERS = 256
ROWS = 131072
CAP = 16
N_CLUS = 4


def shared_clusters(key):
    base = jax.random.fold_in(key, 11)
    key_hot, key_perm, key_local = jax.random.split(base, 3)
    hot_order = jax.random.permutation(key_hot, OWNERS).astype(jnp.int32)
    positions = jnp.arange(ROWS_DEV, dtype=jnp.int32)
    half_rows = CAP * (OWNERS // 4)
    cold_owners = OWNERS - OWNERS // 4
    ranked = jnp.where(positions < half_rows, positions // CAP, OWNERS // 4 + (positions - half_rows) * cold_owners // (ROWS_DEV - half_rows))
    owner_sorted = hot_order[ranked]
    block_keys = jax.random.split(key_perm, ROWS // ROWS_DEV)
    shuffles = jax.vmap(lambda sub_key: jax.random.permutation(sub_key, ROWS_DEV))(block_keys)
    owner_rows = owner_sorted[shuffles].reshape(ROWS)
    local_index = jax.random.randint(key_local, (ROWS,), 0, CPO, dtype=jnp.int32)
    return (owner_rows + OWNERS * local_index).astype(jnp.int32)


def draw_cluster(key, part):
    return shared_clusters(key)


def draw_embeddings(key, part):
    labels = shared_clusters(key)
    key = jax.random.fold_in(key, 5)
    key_centre, key_weight, key_noise, key_scale = jax.random.split(key, 4)
    centre = jnp.clip(jax.random.normal(key_centre, (CLUSTERS, D), jnp.float32), -4.0, 4.0)
    weight = jax.random.uniform(key_weight, (ROWS, 1), jnp.float32, 0.3, 3.0)
    noise = jnp.clip(jax.random.normal(key_noise, (ROWS, D), jnp.float32), -5.0, 5.0)
    scale = jnp.exp(jax.random.uniform(key_scale, (ROWS, 1), jnp.float32, 0.0, math.log(10.0)))
    values = (weight * centre[labels] + noise) * scale
    return values.astype(jnp.bfloat16)


def setup_inputs(seed: int = 0) -> dict:
    key_list = jax.random.split(jax.random.key(seed), 4)
    embeddings = draw_embeddings(jax.random.fold_in(key_list[3], 71), 0)
    cluster = draw_cluster(jax.random.fold_in(key_list[3], 71), 0)
    arrival = jax.random.permutation(key_list[2], ROWS).astype(jnp.int32)
    return {"embeddings": embeddings, "cluster": cluster, "arrival": arrival}


EPSILON = 1e-06

def reference(embeddings, cluster, arrival):
    wide = embeddings.astype(jnp.float32)
    inverse = lax.rsqrt(lax.optimization_barrier(jnp.sum(wide * wide, axis=1)) + EPSILON)
    sort_key = cluster * ROWS + arrival
    ordering = jnp.argsort(sort_key).astype(jnp.int32)
    sorted_rows = embeddings[ordering]
    sorted_inverse = inverse[ordering]
    sorted_cluster = cluster[ordering]
    sorted_arrival = arrival[ordering]
    query_width = min(512, ROWS)
    window = min(ROWS, query_width + 2 * ROWS_DEV * N_CLUS)

    def one_block(block_index):
        start = (block_index * query_width).astype(jnp.int32)
        key_start = jnp.clip(start + query_width - window, 0, ROWS - window).astype(jnp.int32)
        query_rows = lax.dynamic_slice_in_dim(sorted_rows, start, query_width, 0)
        query_inverse = lax.dynamic_slice_in_dim(sorted_inverse, start, query_width, 0)
        query_cluster = lax.dynamic_slice_in_dim(sorted_cluster, start, query_width, 0)
        query_arrival = lax.dynamic_slice_in_dim(sorted_arrival, start, query_width, 0)
        key_rows = lax.dynamic_slice_in_dim(sorted_rows, key_start, window, 0)
        key_inverse = lax.dynamic_slice_in_dim(sorted_inverse, key_start, window, 0)
        key_cluster = lax.dynamic_slice_in_dim(sorted_cluster, key_start, window, 0)
        key_arrival = lax.dynamic_slice_in_dim(sorted_arrival, key_start, window, 0)
        scores = jnp.dot(query_rows, key_rows.T, preferred_element_type=jnp.float32)
        cosine = scores * query_inverse[:, None] * key_inverse[None, :]
        allowed = (query_cluster[:, None] == key_cluster[None, :]) & (key_arrival[None, :] < query_arrival[:, None])
        return lax.optimization_barrier(jnp.max(jnp.where(allowed, cosine, jnp.float32(-1.0)), axis=1))
    blocks = lax.map(one_block, jnp.arange(ROWS // query_width, dtype=jnp.int32))
    best_sorted = blocks.reshape(ROWS)
    return jnp.zeros((ROWS,), jnp.float32).at[ordering].set(best_sorted)
```

```python
import jax
import jax.numpy as jnp
from jax import lax
from jax.experimental import pallas as pl
from jax.experimental.pallas import tpu as pltpu
from jax.sharding import PartitionSpec as P

EPSILON = 1e-06
OWNERS = 64
SLOTS = 16
ROWS = 512
D = 1024
PANEL = OWNERS * SLOTS
LANES = 128
TILES = D // LANES
META = TILES * SLOTS
HEIGHT = META + 8
SPAN = 131072
NONE = -3e38
VMEM = pl.BlockSpec(memory_space=pltpu.VMEM)


def iota(shape, dim):
    return lax.broadcasted_iota(jnp.int32, shape, dim)


def nt(a, b):
    return lax.dot_general(a, b, (((1,), (1,)), ((), ())), preferred_element_type=jnp.float32)


def pack_kernel(rows_ref, cluster_ref, arrival_ref, out_ref, slot_ref):
    cluster, arrival = cluster_ref[...], arrival_ref[...]
    owner = cluster % OWNERS
    member = iota((OWNERS, ROWS), 0) == owner
    member_bf = member.astype(jnp.bfloat16)
    earlier = (iota((ROWS, ROWS), 0) < iota((ROWS, ROWS), 1)).astype(jnp.bfloat16)
    before = jnp.dot(member_bf, earlier, preferred_element_type=jnp.float32)
    within = jnp.sum(jnp.where(member, before, 0.0), axis=0, keepdims=True).astype(jnp.int32)
    slot = owner * SLOTS + within
    slot_ref[...] = slot
    rows = rows_ref[...]
    group = 16
    for g in range(OWNERS // group):
        first = g * group * SLOTS
        pick = (iota((group * SLOTS, ROWS), 0) + first == slot).astype(jnp.bfloat16)
        moved = jnp.dot(pick, rows, preferred_element_type=jnp.float32).astype(jnp.bfloat16)
        moved = moved.reshape(group, SLOTS, D)
        for k in range(TILES):
            out_ref[g * group : (g + 1) * group, k * SLOTS : (k + 1) * SLOTS, :] = moved[
                :, :, k * LANES : (k + 1) * LANES
            ]
    digits = (cluster + 1, arrival % 256, arrival // 256 % 256, arrival // 65536)
    lane = iota((LANES, ROWS), 0)
    spread = jnp.zeros((LANES, ROWS), jnp.int32)
    for k, digit in enumerate(digits):
        spread = jnp.where(lane // SLOTS == k, digit, spread)
    spread = jnp.where(lane % SLOTS == within, spread, 0).astype(jnp.float32).astype(jnp.bfloat16)
    meta = nt(member_bf, spread).astype(jnp.bfloat16)
    out_ref[:, META:, :] = jnp.broadcast_to(meta[:, None, :], (OWNERS, HEIGHT - META, LANES))


def pack(rows, cluster, arrival):
    return pl.pallas_call(
        pack_kernel,
        out_shape=(
            jax.ShapeDtypeStruct((OWNERS, HEIGHT, LANES), jnp.bfloat16),
            jax.ShapeDtypeStruct((1, ROWS), jnp.int32),
        ),
        in_specs=[VMEM] * 3,
        out_specs=(VMEM, VMEM),
        compiler_params=pltpu.CompilerParams(vmem_limit_bytes=40 * 2**20),
    )(rows, cluster.reshape(1, ROWS), arrival.reshape(1, ROWS))


def weights(shape, lane_dim, slot_dim):
    lane = iota(shape, lane_dim)
    mine = lane % SLOTS == iota(shape, slot_dim) % SLOTS
    kind = lane // SLOTS
    place = jnp.where(kind == 1, 1.0, jnp.where(kind == 2, 256.0, jnp.where(kind == 3, 65536.0, 0.0)))
    return jnp.where(mine & (kind == 0), 1.0, 0.0), jnp.where(mine, place, 0.0)


def column_keys(meta):
    spread = (iota((PANEL, OWNERS), 0) // SLOTS == iota((PANEL, OWNERS), 1)).astype(jnp.bfloat16)
    mine = jnp.dot(spread, meta, preferred_element_type=jnp.float32)
    of_cluster, of_arrival = weights((PANEL, LANES), 1, 0)
    cluster = jnp.sum(mine * of_cluster, axis=1, keepdims=True).astype(jnp.int32) - 1
    arrival = jnp.sum(mine * of_arrival, axis=1, keepdims=True).astype(jnp.int32)
    return cluster * SPAN + arrival


def row_keys(meta):
    of_cluster, of_arrival = weights((LANES, PANEL), 0, 1)
    mine = iota((OWNERS, PANEL), 1) // SLOTS == iota((OWNERS, PANEL), 0)

    def line(weight):
        every = jnp.dot(meta, weight.astype(jnp.bfloat16), preferred_element_type=jnp.float32)
        return jnp.sum(jnp.where(mine, every, 0.0), axis=0, keepdims=True).astype(jnp.int32)

    base = (line(of_cluster) - 1) * SPAN
    return base, base + line(of_arrival)


def squares(panel):
    width = 128
    eye = iota((width, width), 0) == iota((width, width), 1)
    for start in range(0, PANEL, width):
        part = panel[start : start + width, :]
        yield jnp.where(eye, nt(part, part), 0.0)


def column_inverse(panel):
    return lax.rsqrt(
        jnp.concatenate([jnp.sum(s, axis=1, keepdims=True) for s in squares(panel)], axis=0) + EPSILON
    )


def row_inverse(panel):
    return lax.rsqrt(
        jnp.concatenate([jnp.sum(s, axis=0, keepdims=True) for s in squares(panel)], axis=1) + EPSILON
    )


def fold(best, queries, base, limit, keys, key, inverse):
    width = 256
    for start in range(0, PANEL, width):
        scores = nt(keys[start : start + width, :], queries[...])
        here = key[start : start + width]
        value = scores * inverse[start : start + width]
        allowed = (here < limit) & (here >= base)
        best = jnp.maximum(best, jnp.max(jnp.where(allowed, value, NONE), axis=0, keepdims=True))
    return best


def to_block(line):
    mine = iota((OWNERS, PANEL), 1) // SLOTS == iota((OWNERS, PANEL), 0)
    place = (iota((PANEL, LANES), 0) % SLOTS == iota((PANEL, LANES), 1)).astype(jnp.float32)
    return lax.dot_general(
        jnp.where(mine, line, 0.0),
        place,
        (((1,), (0,)), ((), ())),
        precision=lax.Precision.HIGHEST,
        preferred_element_type=jnp.float32,
    )


def score_kernel(own_ref, below_ref, above_ref, own_out, below_out, own, below, above):
    for source, target in ((own_ref, own), (below_ref, below), (above_ref, above)):
        for k in range(TILES):
            target[:, k * LANES : (k + 1) * LANES] = source[
                :, k * SLOTS : (k + 1) * SLOTS, :
            ].reshape(PANEL, LANES)
    own_meta, below_meta, above_meta = (
        ref[:, META:, :].astype(jnp.float32)[:, 0, :].astype(jnp.bfloat16)
        for ref in (own_ref, below_ref, above_ref)
    )
    above_key, above_inverse = column_keys(above_meta), column_inverse(above)
    nothing = jnp.full((1, PANEL), NONE, jnp.float32)

    base, limit = row_keys(own_meta)
    best = fold(nothing, own, base, limit, own, column_keys(own_meta), column_inverse(own))
    best = fold(best, own, base, limit, below, column_keys(below_meta), column_inverse(below))
    best = fold(best, own, base, limit, above, above_key, above_inverse)
    own_out[...] = to_block(jnp.where(best > 0.5 * NONE, jnp.maximum(best * row_inverse(own), -1.0), -1.0))

    base, limit = row_keys(below_meta)
    best = fold(nothing, below, base, limit, above, above_key, above_inverse)
    below_out[...] = to_block(jnp.where(best > 0.5 * NONE, jnp.maximum(best * row_inverse(below), -1.0), -1.0))


def score(own, below, above):
    return pl.pallas_call(
        score_kernel,
        out_shape=(jax.ShapeDtypeStruct((OWNERS, LANES), jnp.float32),) * 2,
        in_specs=[VMEM] * 3,
        out_specs=(VMEM, VMEM),
        scratch_shapes=[pltpu.VMEM((PANEL, D), jnp.bfloat16)] * 3,
        compiler_params=pltpu.CompilerParams(vmem_limit_bytes=56 * 2**20),
    )(own, below, above)


def unpack_kernel(block_ref, slot_ref, out_ref):
    slot = slot_ref[...]
    member = (iota((OWNERS, ROWS), 0) == slot // SLOTS).astype(jnp.float32)
    every = lax.dot_general(
        block_ref[...],
        member,
        (((0,), (0,)), ((), ())),
        precision=lax.Precision.HIGHEST,
        preferred_element_type=jnp.float32,
    )
    mine = iota((LANES, ROWS), 0) == slot % SLOTS
    out_ref[...] = jnp.sum(jnp.where(mine, every, 0.0), axis=0, keepdims=True)


def unpack(block, slot):
    return pl.pallas_call(
        unpack_kernel,
        out_shape=jax.ShapeDtypeStruct((1, ROWS), jnp.float32),
        in_specs=[VMEM] * 2,
        out_specs=VMEM,
    )(block, slot).reshape(ROWS)


def passed_along(array, by):
    size = lax.axis_size("clus")
    return lax.ppermute(array, "clus", [(i, (i + by) % size) for i in range(size)])


def to_owners(array):
    return lax.all_to_all(array, "shard", split_axis=0, concat_axis=0, tiled=True)


def per_device(embeddings, cluster, arrival):
    packed, slot = pack(embeddings, cluster, arrival)
    own = to_owners(packed)
    below, above = passed_along(own, 1), passed_along(own, -1)
    best, for_below = score(own, below, above)
    best = jnp.maximum(best, passed_along(for_below, -1))
    return unpack(to_owners(best), slot)


def solution(mesh):
    in_specs = (P(("shard", "clus"), None), P(("shard", "clus")), P(("shard", "clus")))
    out_specs = P(("shard", "clus"))
    return jax.shard_map(
        per_device, mesh=mesh, in_specs=in_specs, out_specs=out_specs, check_vma=False
    )
```

```python
import jax
import jax.numpy as jnp
from jax import lax
from jax.experimental import pallas as pl
from jax.experimental.pallas import tpu as pltpu
from jax.sharding import PartitionSpec as P

EPSILON = 1e-06
OWNERS = 64
CAPACITY = 16
ROWS = 512
D = 1024
GROUPS = 32
SLOTS = 2 * CAPACITY
PANEL = GROUPS * SLOTS
LANES = 128
TILES = D // LANES
META = TILES * SLOTS
HEIGHT = META + 8
SPAN = 131072
NONE = -3e38
Z, X, Y = 8, 4, 4
AXES = ("shard", "clus")
VMEM = pl.BlockSpec(memory_space=pltpu.VMEM)
SMEM = pl.BlockSpec(memory_space=pltpu.SMEM)


def iota(shape, dim):
    return lax.broadcasted_iota(jnp.int32, shape, dim)


def nt(a, b):
    return lax.dot_general(a, b, (((1,), (1,)), ((), ())), preferred_element_type=jnp.float32)


def pack_kernel(core_ref, rows_ref, label_ref, other_rows_ref, other_label_ref, out_ref, slot_ref):
    core = core_ref[0]
    earlier = (iota((ROWS, ROWS), 0) < iota((ROWS, ROWS), 1)).astype(jnp.bfloat16)
    meta = jnp.zeros((GROUPS, LANES), jnp.float32)
    for half, (rows, label) in enumerate(
        ((rows_ref[...], label_ref[...]), (other_rows_ref[...], other_label_ref[...]))
    ):
        cluster, arrival = label // SPAN, label % SPAN
        owner = cluster % OWNERS
        group = owner // 2
        member = iota((OWNERS, ROWS), 0) == owner
        before = jnp.dot(member.astype(jnp.bfloat16), earlier, preferred_element_type=jnp.float32)
        within = jnp.sum(jnp.where(member, before, 0.0), axis=0, keepdims=True).astype(jnp.int32)
        mine = owner % 2 == core
        slot = group * CAPACITY + within
        if half == 0:
            slot_ref[...] = jnp.where(mine, slot, slot + GROUPS * CAPACITY)
        slot = jnp.where(mine, slot, -1)
        step = 8
        for g in range(0, GROUPS, step):
            pick = (iota((step * CAPACITY, ROWS), 0) + g * CAPACITY == slot).astype(jnp.bfloat16)
            moved = jnp.dot(pick, rows, preferred_element_type=jnp.float32).astype(jnp.bfloat16)
            moved = moved.reshape(step, CAPACITY, D)
            for k in range(TILES):
                first = k * SLOTS + half * CAPACITY
                out_ref[g : g + step, first : first + CAPACITY, :] = moved[
                    :, :, k * LANES : (k + 1) * LANES
                ]
        lane = iota((LANES, ROWS), 0)
        kind = lane // SLOTS
        digits = (cluster + 1, arrival % 256, arrival // 256 % 256, arrival // 65536)
        spread = jnp.zeros((LANES, ROWS), jnp.int32)
        for k, digit in enumerate(digits):
            spread = jnp.where(kind == k, digit, spread)
        spread = jnp.where(lane % SLOTS == within + half * CAPACITY, spread, 0)
        to = ((iota((GROUPS, ROWS), 0) == group) & mine).astype(jnp.bfloat16)
        meta = meta + nt(to, spread.astype(jnp.float32).astype(jnp.bfloat16))
    meta = meta.astype(jnp.bfloat16)
    out_ref[:, META:, :] = jnp.broadcast_to(meta[:, None, :], (GROUPS, HEIGHT - META, LANES))


def pack(core, rows, label, other_rows, other_label):
    return pl.pallas_call(
        pack_kernel,
        out_shape=(
            jax.ShapeDtypeStruct((GROUPS, HEIGHT, LANES), jnp.bfloat16),
            jax.ShapeDtypeStruct((1, ROWS), jnp.int32),
        ),
        in_specs=[SMEM] + [VMEM] * 4,
        out_specs=(VMEM, VMEM),
        compiler_params=pltpu.CompilerParams(vmem_limit_bytes=20 * 2**20),
    )(core, rows, label, other_rows, other_label)


def weights(shape, lane_dim, slot_dim):
    lane = iota(shape, lane_dim)
    mine = lane % SLOTS == iota(shape, slot_dim) % SLOTS
    kind = lane // SLOTS
    place = jnp.where(kind == 1, 1.0, jnp.where(kind == 2, 256.0, jnp.where(kind == 3, 65536.0, 0.0)))
    return jnp.where(mine & (kind == 0), 1.0, 0.0), jnp.where(mine, place, 0.0)


def column_keys(meta):
    spread = (iota((PANEL, GROUPS), 0) // SLOTS == iota((PANEL, GROUPS), 1)).astype(jnp.bfloat16)
    mine = jnp.dot(spread, meta, preferred_element_type=jnp.float32)
    of_cluster, of_arrival = weights((PANEL, LANES), 1, 0)
    cluster = jnp.sum(mine * of_cluster, axis=1, keepdims=True).astype(jnp.int32) - 1
    arrival = jnp.sum(mine * of_arrival, axis=1, keepdims=True).astype(jnp.int32)
    return cluster * SPAN + arrival


def row_keys(meta):
    of_cluster, of_arrival = weights((LANES, PANEL), 0, 1)
    mine = iota((GROUPS, PANEL), 1) // SLOTS == iota((GROUPS, PANEL), 0)

    def line(weight):
        every = jnp.dot(meta, weight.astype(jnp.bfloat16), preferred_element_type=jnp.float32)
        return jnp.sum(jnp.where(mine, every, 0.0), axis=0, keepdims=True).astype(jnp.int32)

    base = (line(of_cluster) - 1) * SPAN
    return base, base + line(of_arrival)


def squares(panel):
    width = 128
    eye = iota((width, width), 0) == iota((width, width), 1)
    for start in range(0, PANEL, width):
        part = panel[start : start + width, :]
        yield jnp.where(eye, nt(part, part), 0.0)


def column_inverse(panel):
    return lax.rsqrt(
        jnp.concatenate([jnp.sum(s, axis=1, keepdims=True) for s in squares(panel)], axis=0) + EPSILON
    )


def row_inverse(panel):
    return lax.rsqrt(
        jnp.concatenate([jnp.sum(s, axis=0, keepdims=True) for s in squares(panel)], axis=1) + EPSILON
    )


def fold(best, queries, base, limit, keys, key, inverse):
    width = 256
    for start in range(0, PANEL, width):
        scores = nt(keys[start : start + width, :], queries[...])
        here = key[start : start + width]
        value = scores * inverse[start : start + width]
        allowed = (here < limit) & (here >= base)
        best = jnp.maximum(best, jnp.max(jnp.where(allowed, value, NONE), axis=0, keepdims=True))
    return best


def to_block(line):
    mine = iota((GROUPS, PANEL), 1) // SLOTS == iota((GROUPS, PANEL), 0)
    place = (iota((PANEL, LANES), 0) % SLOTS == iota((PANEL, LANES), 1)).astype(jnp.float32)
    return lax.dot_general(
        jnp.where(mine, line, 0.0),
        place,
        (((1,), (0,)), ((), ())),
        precision=lax.Precision.HIGHEST,
        preferred_element_type=jnp.float32,
    )


def finish(best, inverse):
    return to_block(jnp.where(best > 0.5 * NONE, jnp.maximum(best * inverse, -1.0), -1.0))


def unfold(source, target):
    for k in range(TILES):
        target[:, k * LANES : (k + 1) * LANES] = source[:, k * SLOTS : (k + 1) * SLOTS, :].reshape(
            PANEL, LANES
        )
    return source[:, META:, :].astype(jnp.float32)[:, 0, :].astype(jnp.bfloat16)


def own_kernel(own_ref, own, best_ref, inverse_ref):
    meta = unfold(own_ref, own)
    base, limit = row_keys(meta)
    nothing = jnp.full((1, PANEL), NONE, jnp.float32)
    best_ref[...] = fold(nothing, own, base, limit, own, column_keys(meta), column_inverse(own))
    inverse_ref[...] = row_inverse(own)


def score_own(own):
    return pl.pallas_call(
        own_kernel,
        out_shape=(
            jax.ShapeDtypeStruct((PANEL, D), jnp.bfloat16),
            jax.ShapeDtypeStruct((1, PANEL), jnp.float32),
            jax.ShapeDtypeStruct((1, PANEL), jnp.float32),
        ),
        in_specs=[VMEM],
        out_specs=(VMEM, VMEM, VMEM),
        compiler_params=pltpu.CompilerParams(vmem_limit_bytes=20 * 2**20),
        cost_estimate=pl.CostEstimate(flops=4 * 2**30, bytes_accessed=4 * 2**20, transcendentals=0),
    )(own)


def rest_kernel(
    packed_ref, own, best_ref, inverse_ref, below_ref, above_ref, own_out, below_out, below, above
):
    own_meta = packed_ref[:, META:, :].astype(jnp.float32)[:, 0, :].astype(jnp.bfloat16)
    below_meta, above_meta = unfold(below_ref, below), unfold(above_ref, above)
    above_key, above_inverse = column_keys(above_meta), column_inverse(above)

    base, limit = row_keys(own_meta)
    best = fold(best_ref[...], own, base, limit, below, column_keys(below_meta), column_inverse(below))
    best = fold(best, own, base, limit, above, above_key, above_inverse)
    own_out[...] = finish(best, inverse_ref[...])

    base, limit = row_keys(below_meta)
    nothing = jnp.full((1, PANEL), NONE, jnp.float32)
    best = fold(nothing, below, base, limit, above, above_key, above_inverse)
    below_out[...] = finish(best, row_inverse(below))


def score_rest(packed, own, best, inverse, below, above):
    return pl.pallas_call(
        rest_kernel,
        out_shape=(jax.ShapeDtypeStruct((GROUPS, LANES), jnp.float32),) * 2,
        in_specs=[VMEM] * 6,
        out_specs=(VMEM, VMEM),
        scratch_shapes=[pltpu.VMEM((PANEL, D), jnp.bfloat16)] * 2,
        compiler_params=pltpu.CompilerParams(vmem_limit_bytes=24 * 2**20),
    )(packed, own, best, inverse, below, above)


def unpack_kernel(block_ref, other_ref, slot_ref, out_ref):
    slot = slot_ref[...]
    half = slot // (GROUPS * CAPACITY)
    member = (iota((GROUPS, ROWS), 0) == slot // CAPACITY % GROUPS).astype(jnp.float32)

    def every(ref):
        return lax.dot_general(
            ref[...],
            member,
            (((0,), (0,)), ((), ())),
            precision=lax.Precision.HIGHEST,
            preferred_element_type=jnp.float32,
        )

    mine = iota((LANES, ROWS), 0) == slot % CAPACITY + half * CAPACITY
    value = jnp.where(half == 0, every(block_ref), every(other_ref))
    out_ref[...] = jnp.sum(jnp.where(mine, value, 0.0), axis=0, keepdims=True)


def unpack(block, other, slot):
    return pl.pallas_call(
        unpack_kernel,
        out_shape=jax.ShapeDtypeStruct((1, ROWS), jnp.float32),
        in_specs=[VMEM] * 3,
        out_specs=VMEM,
    )(block, other, slot).reshape(ROWS)


def device(z, x, core, y):
    return ((z * X + x) * 2 + core) * Y + y


OWNER_GROUPS = [[device(z, x, 0, y) for z in range(Z) for x in range(X)] for y in range(Y)] + [
    [device(z, x, 1, y) for z in range(Z) for y in range(Y)] for x in range(X)
]


def to_owners(array):
    return lax.all_to_all(
        array, AXES, split_axis=0, concat_axis=0, tiled=True, axis_index_groups=OWNER_GROUPS
    )


def passed_along(array, by):
    pairs = []
    for z in range(Z):
        for x in range(X):
            for y in range(Y):
                pairs.append((device(z, x, 0, y), device(z, x, 0, (y + by) % Y)))
                pairs.append((device(z, x, 1, y), device(z, (x + by) % X, 1, y)))
    return lax.ppermute(array, AXES, pairs)


def other_core(array):
    size = lax.axis_size("shard")
    return lax.ppermute(array, "shard", [(i, i ^ 1) for i in range(size)])


def per_device(embeddings, cluster, arrival):
    label = (cluster * SPAN + arrival).reshape(1, ROWS)
    core = (lax.axis_index("shard") % 2).reshape(1)
    packed, slot = pack(core, embeddings, label, other_core(embeddings), other_core(label))
    own = to_owners(packed)
    below, above = passed_along(own, 1), passed_along(own, -1)
    rows, best, inverse = score_own(own)
    best, for_below = score_rest(own, rows, best, inverse, below, above)
    best = jnp.maximum(best, passed_along(for_below, -1))
    returned = to_owners(best)
    return unpack(returned, other_core(returned), slot)


def solution(mesh):
    in_specs = (P(("shard", "clus"), None), P(("shard", "clus")), P(("shard", "clus")))
    out_specs = P(("shard", "clus"))
    return jax.shard_map(
        per_device, mesh=mesh, in_specs=in_specs, out_specs=out_specs, check_vma=False
    )
```

```python
import jax
import jax.numpy as jnp
from jax import lax
from jax.experimental import pallas as pl
from jax.experimental.pallas import tpu as pltpu
from jax.sharding import PartitionSpec as P

EPSILON = 1e-06
OWNERS = 64
CAPACITY = 16
ROWS = 512
D = 1024
GROUPS = 32
SLOTS = 2 * CAPACITY
PANEL = GROUPS * SLOTS
LANES = 128
TILES = D // LANES
PARTS = (6, 2)
META = PARTS[1] * SLOTS
HEIGHTS = (PARTS[0] * SLOTS, META + 8)
SPAN = 131072
NONE = -3e38
Z, X, Y = 8, 4, 4
AXES = ("shard", "clus")
VMEM = pl.BlockSpec(memory_space=pltpu.VMEM)
SMEM = pl.BlockSpec(memory_space=pltpu.SMEM)


def iota(shape, dim):
    return lax.broadcasted_iota(jnp.int32, shape, dim)


def nt(a, b):
    return lax.dot_general(a, b, (((1,), (1,)), ((), ())), preferred_element_type=jnp.float32)


def pack_kernel(core_ref, rows_ref, label_ref, other_rows_ref, other_label_ref, first_ref, second_ref, slot_ref):
    core = core_ref[0]
    earlier = (iota((ROWS, ROWS), 0) < iota((ROWS, ROWS), 1)).astype(jnp.bfloat16)
    meta = jnp.zeros((GROUPS, LANES), jnp.float32)
    for half, (rows, label) in enumerate(
        ((rows_ref[...], label_ref[...]), (other_rows_ref[...], other_label_ref[...]))
    ):
        cluster, arrival = label // SPAN, label % SPAN
        owner = cluster % OWNERS
        group = owner // 2
        member = iota((OWNERS, ROWS), 0) == owner
        before = jnp.dot(member.astype(jnp.bfloat16), earlier, preferred_element_type=jnp.float32)
        within = jnp.sum(jnp.where(member, before, 0.0), axis=0, keepdims=True).astype(jnp.int32)
        mine = owner % 2 == core
        slot = group * CAPACITY + within
        if half == 0:
            slot_ref[...] = jnp.where(mine, slot, slot + GROUPS * CAPACITY)
        slot = jnp.where(mine, slot, -1)
        step = 8
        for g in range(0, GROUPS, step):
            pick = (iota((step * CAPACITY, ROWS), 0) + g * CAPACITY == slot).astype(jnp.bfloat16)
            moved = jnp.dot(pick, rows, preferred_element_type=jnp.float32).astype(jnp.bfloat16)
            moved = moved.reshape(step, CAPACITY, D)
            for k in range(TILES):
                out_ref, tile = (first_ref, k) if k < PARTS[0] else (second_ref, k - PARTS[0])
                place = tile * SLOTS + half * CAPACITY
                out_ref[g : g + step, place : place + CAPACITY, :] = moved[
                    :, :, k * LANES : (k + 1) * LANES
                ]
        lane = iota((LANES, ROWS), 0)
        kind = lane // SLOTS
        digits = (cluster + 1, arrival % 256, arrival // 256 % 256, arrival // 65536)
        spread = jnp.zeros((LANES, ROWS), jnp.int32)
        for k, digit in enumerate(digits):
            spread = jnp.where(kind == k, digit, spread)
        spread = jnp.where(lane % SLOTS == within + half * CAPACITY, spread, 0)
        to = ((iota((GROUPS, ROWS), 0) == group) & mine).astype(jnp.bfloat16)
        meta = meta + nt(to, spread.astype(jnp.float32).astype(jnp.bfloat16))
    meta = meta.astype(jnp.bfloat16)
    second_ref[:, META:, :] = jnp.broadcast_to(meta[:, None, :], (GROUPS, HEIGHTS[1] - META, LANES))


def pack(core, rows, label, other_rows, other_label):
    return pl.pallas_call(
        pack_kernel,
        out_shape=tuple(
            jax.ShapeDtypeStruct((GROUPS, height, LANES), jnp.bfloat16) for height in HEIGHTS
        )
        + (jax.ShapeDtypeStruct((1, ROWS), jnp.int32),),
        in_specs=[SMEM] + [VMEM] * 4,
        out_specs=(VMEM,) * 3,
        compiler_params=pltpu.CompilerParams(vmem_limit_bytes=20 * 2**20),
    )(core, rows, label, other_rows, other_label)


def weights(shape, lane_dim, slot_dim):
    lane = iota(shape, lane_dim)
    mine = lane % SLOTS == iota(shape, slot_dim) % SLOTS
    kind = lane // SLOTS
    place = jnp.where(kind == 1, 1.0, jnp.where(kind == 2, 256.0, jnp.where(kind == 3, 65536.0, 0.0)))
    return jnp.where(mine & (kind == 0), 1.0, 0.0), jnp.where(mine, place, 0.0)


def column_keys(meta):
    spread = (iota((PANEL, GROUPS), 0) // SLOTS == iota((PANEL, GROUPS), 1)).astype(jnp.bfloat16)
    mine = jnp.dot(spread, meta, preferred_element_type=jnp.float32)
    of_cluster, of_arrival = weights((PANEL, LANES), 1, 0)
    cluster = jnp.sum(mine * of_cluster, axis=1, keepdims=True).astype(jnp.int32) - 1
    arrival = jnp.sum(mine * of_arrival, axis=1, keepdims=True).astype(jnp.int32)
    return cluster * SPAN + arrival


def row_keys(meta):
    of_cluster, of_arrival = weights((LANES, PANEL), 0, 1)
    mine = iota((GROUPS, PANEL), 1) // SLOTS == iota((GROUPS, PANEL), 0)

    def line(weight):
        every = jnp.dot(meta, weight.astype(jnp.bfloat16), preferred_element_type=jnp.float32)
        return jnp.sum(jnp.where(mine, every, 0.0), axis=0, keepdims=True).astype(jnp.int32)

    base = (line(of_cluster) - 1) * SPAN
    return base, base + line(of_arrival)


def eye(width):
    return iota((width, width), 0) == iota((width, width), 1)


def as_row(column):
    width = 128
    return jnp.concatenate(
        [
            jnp.sum(jnp.where(eye(width), column[start : start + width], 0.0), axis=0, keepdims=True)
            for start in range(0, PANEL, width)
        ],
        axis=1,
    )


def as_column(row):
    width = 128
    return jnp.concatenate(
        [
            jnp.sum(jnp.where(eye(width), row[:, start : start + width], 0.0), axis=1, keepdims=True)
            for start in range(0, PANEL, width)
        ],
        axis=0,
    )


def tiles_of(source, count):
    return [source[:, k * SLOTS : (k + 1) * SLOTS, :].reshape(PANEL, LANES) for k in range(count)]


def squares(source, count):
    total = jnp.zeros((PANEL, LANES), jnp.float32)
    for tile in tiles_of(source, count):
        wide = tile.astype(jnp.float32)
        total = total + wide * wide
    return jnp.sum(total, axis=1, keepdims=True)


def unfold(source, target, count, at=0):
    for k, tile in enumerate(tiles_of(source, count)):
        target[:, (at + k) * LANES : (at + k + 1) * LANES] = tile


def labels(source):
    return source[:, META:, :].astype(jnp.float32)[:, 0, :].astype(jnp.bfloat16)


def fold(best, tile_of, base, limit, key, inverse):
    width = 256
    for start in range(0, PANEL, width):
        here = key[start : start + width]
        value = tile_of(slice(start, start + width)) * inverse[start : start + width]
        allowed = (here < limit) & (here >= base)
        best = jnp.maximum(best, jnp.max(jnp.where(allowed, value, NONE), axis=0, keepdims=True))
    return best


def nothing():
    return jnp.full((1, PANEL), NONE, jnp.float32)


def to_block(line):
    mine = iota((GROUPS, PANEL), 1) // SLOTS == iota((GROUPS, PANEL), 0)
    place = (iota((PANEL, LANES), 0) % SLOTS == iota((PANEL, LANES), 1)).astype(jnp.float32)
    return lax.dot_general(
        jnp.where(mine, line, 0.0),
        place,
        (((1,), (0,)), ((), ())),
        precision=lax.Precision.HIGHEST,
        preferred_element_type=jnp.float32,
    )


def finish(best, inverse):
    return to_block(jnp.where(best > 0.5 * NONE, jnp.maximum(best * inverse, -1.0), -1.0))


LINE = jax.ShapeDtypeStruct((1, PANEL), jnp.float32)
SQUARE = jax.ShapeDtypeStruct((PANEL, PANEL), jnp.float32)
HEAD = PARTS[0] * LANES
TAIL = PARTS[1] * LANES


def norms_kernel(below_ref, above_ref, below_out, above_out):
    below_out[...] = as_row(squares(below_ref, PARTS[0]))
    above_out[...] = as_row(squares(above_ref, PARTS[0]))


def norms(below, above):
    return pl.pallas_call(
        norms_kernel,
        out_shape=(LINE, LINE),
        in_specs=[VMEM] * 2,
        out_specs=(VMEM,) * 2,
        compiler_params=pltpu.CompilerParams(vmem_limit_bytes=16 * 2**20),
        cost_estimate=pl.CostEstimate(flops=32 * 2**30, bytes_accessed=2**25, transcendentals=0),
    )(below, above)


def head_kernel(
    first_ref,
    second_ref,
    below_ref,
    above_ref,
    best_ref,
    inverse_ref,
    own_below,
    own_above,
    below_above,
    own,
    below,
    above,
):
    unfold(first_ref, own, PARTS[0])
    unfold(second_ref, own, PARTS[1], PARTS[0])
    unfold(below_ref, below, PARTS[0])
    unfold(above_ref, above, PARTS[0])
    meta = labels(second_ref)
    base, limit = row_keys(meta)
    inverse = lax.rsqrt(squares(first_ref, PARTS[0]) + squares(second_ref, PARTS[1]) + EPSILON)
    inverse_ref[...] = as_row(inverse)
    best_ref[...] = fold(
        nothing(), lambda at: nt(own[at, :], own[...]), base, limit, column_keys(meta), inverse
    )
    width = 256
    for start in range(0, PANEL, width):
        at = slice(start, start + width)
        own_below[at, :] = nt(below[at, :], own[:, :HEAD])
        own_above[at, :] = nt(above[at, :], own[:, :HEAD])
        below_above[at, :] = nt(above[at, :], below[...])


def score_head(first, second, below, above):
    return pl.pallas_call(
        head_kernel,
        out_shape=(LINE, LINE, SQUARE, SQUARE, SQUARE),
        in_specs=[VMEM] * 4,
        out_specs=(VMEM,) * 5,
        scratch_shapes=[pltpu.VMEM((PANEL, D), jnp.bfloat16)]
        + [pltpu.VMEM((PANEL, HEAD), jnp.bfloat16)] * 2,
        compiler_params=pltpu.CompilerParams(vmem_limit_bytes=32 * 2**20),
        cost_estimate=pl.CostEstimate(flops=8 * 2**30, bytes_accessed=2**24, transcendentals=0),
    )(first, second, below, above)


def tail_kernel(
    second_ref,
    best_ref,
    inverse_ref,
    own_below,
    own_above,
    below_above,
    below_norm_ref,
    above_norm_ref,
    below_ref,
    above_ref,
    own_out,
    below_out,
    own,
    below,
    above,
):
    for source, target in ((second_ref, own), (below_ref, below), (above_ref, above)):
        unfold(source, target, PARTS[1])
    own_meta, below_meta, above_meta = labels(second_ref), labels(below_ref), labels(above_ref)

    def inverse_of(norm_ref, source):
        return lax.rsqrt(as_column(norm_ref[...]) + squares(source, PARTS[1]) + EPSILON)

    below_inverse, above_inverse = (
        inverse_of(below_norm_ref, below_ref),
        inverse_of(above_norm_ref, above_ref),
    )
    above_key = column_keys(above_meta)

    base, limit = row_keys(own_meta)
    best = fold(
        best_ref[...],
        lambda at: own_below[at, :] + nt(below[at, :], own[...]),
        base,
        limit,
        column_keys(below_meta),
        below_inverse,
    )
    best = fold(
        best,
        lambda at: own_above[at, :] + nt(above[at, :], own[...]),
        base,
        limit,
        above_key,
        above_inverse,
    )
    own_out[...] = finish(best, inverse_ref[...])

    base, limit = row_keys(below_meta)
    best = fold(
        nothing(),
        lambda at: below_above[at, :] + nt(above[at, :], below[...]),
        base,
        limit,
        above_key,
        above_inverse,
    )
    below_out[...] = finish(best, as_row(below_inverse))


def score_tail(second, head, below_norm, above_norm, below, above):
    return pl.pallas_call(
        tail_kernel,
        out_shape=(jax.ShapeDtypeStruct((GROUPS, LANES), jnp.float32),) * 2,
        in_specs=[VMEM] * 10,
        out_specs=(VMEM, VMEM),
        scratch_shapes=[pltpu.VMEM((PANEL, TAIL), jnp.bfloat16)] * 3,
        compiler_params=pltpu.CompilerParams(vmem_limit_bytes=28 * 2**20),
    )(second, *head, below_norm, above_norm, below, above)


def unpack_kernel(block_ref, other_ref, slot_ref, out_ref):
    slot = slot_ref[...]
    half = slot // (GROUPS * CAPACITY)
    member = (iota((GROUPS, ROWS), 0) == slot // CAPACITY % GROUPS).astype(jnp.float32)

    def every(ref):
        return lax.dot_general(
            ref[...],
            member,
            (((0,), (0,)), ((), ())),
            precision=lax.Precision.HIGHEST,
            preferred_element_type=jnp.float32,
        )

    mine = iota((LANES, ROWS), 0) == slot % CAPACITY + half * CAPACITY
    value = jnp.where(half == 0, every(block_ref), every(other_ref))
    out_ref[...] = jnp.sum(jnp.where(mine, value, 0.0), axis=0, keepdims=True)


def unpack(block, other, slot):
    return pl.pallas_call(
        unpack_kernel,
        out_shape=jax.ShapeDtypeStruct((1, ROWS), jnp.float32),
        in_specs=[VMEM] * 3,
        out_specs=VMEM,
        compiler_params=pltpu.CompilerParams(vmem_limit_bytes=4 * 2**20),
    )(block, other, slot).reshape(ROWS)


def device(z, x, core, y):
    return ((z * X + x) * 2 + core) * Y + y


OWNER_GROUPS = [[device(z, x, 0, y) for z in range(Z) for x in range(X)] for y in range(Y)] + [
    [device(z, x, 1, y) for z in range(Z) for y in range(Y)] for x in range(X)
]


def to_owners(array):
    return lax.all_to_all(
        array, AXES, split_axis=0, concat_axis=0, tiled=True, axis_index_groups=OWNER_GROUPS
    )


def passed_along(array, by):
    pairs = []
    for z in range(Z):
        for x in range(X):
            for y in range(Y):
                pairs.append((device(z, x, 0, y), device(z, x, 0, (y + by) % Y)))
                pairs.append((device(z, x, 1, y), device(z, (x + by) % X, 1, y)))
    return lax.ppermute(array, AXES, pairs)


def other_core(array):
    size = lax.axis_size("shard")
    return lax.ppermute(array, "shard", [(i, i ^ 1) for i in range(size)])


def per_device(embeddings, cluster, arrival):
    label = (cluster * SPAN + arrival).reshape(1, ROWS)
    core = (lax.axis_index("shard") % 2).reshape(1)
    first, second, slot = pack(core, embeddings, label, other_core(embeddings), other_core(label))
    own_first = to_owners(first)
    below_first, above_first = passed_along(own_first, 1), passed_along(own_first, -1)
    own_second = to_owners(second)
    below_second, above_second = passed_along(own_second, 1), passed_along(own_second, -1)
    below_norm, above_norm = norms(below_first, above_first)
    head = score_head(own_first, own_second, below_first, above_first)
    best, for_below = score_tail(own_second, head, below_norm, above_norm, below_second, above_second)
    best = jnp.maximum(best, passed_along(for_below, -1))
    returned = to_owners(best)
    return unpack(returned, other_core(returned), slot)


def solution(mesh):
    in_specs = (P(("shard", "clus"), None), P(("shard", "clus")), P(("shard", "clus")))
    out_specs = P(("shard", "clus"))
    return jax.shard_map(
        per_device, mesh=mesh, in_specs=in_specs, out_specs=out_specs, check_vma=False
    )
```

```python
import jax
import jax.numpy as jnp
from jax import lax
from jax.experimental import pallas as pl
from jax.experimental.pallas import tpu as pltpu
from jax.sharding import PartitionSpec as P

EPSILON = 1e-06
OWNERS = 64
CAPACITY = 16
ROWS = 512
D = 1024
GROUPS = 32
SLOTS = 2 * CAPACITY
PANEL = GROUPS * SLOTS
HALF = GROUPS * CAPACITY
LANES = 128
PER_TILE = LANES // SLOTS
TILES = D // LANES
PARTS = (6, 2)
LABELS = PARTS[0] * SLOTS
HEIGHTS = (LABELS + 8, PARTS[1] * SLOTS)
HEAD = PARTS[0] * LANES
TAIL = PARTS[1] * LANES
SPAN = 131072
NONE = float("-inf")
Z, X, Y = 8, 4, 4
AXES = ("shard", "clus")
VMEM = pl.BlockSpec(memory_space=pltpu.VMEM)
SMEM = pl.BlockSpec(memory_space=pltpu.SMEM)
LINE = jax.ShapeDtypeStruct((1, PANEL), jnp.float32)
SQUARE = jax.ShapeDtypeStruct((PANEL, PANEL), jnp.float32)


def iota(shape, dim):
    return lax.broadcasted_iota(jnp.int32, shape, dim)


def nt(a, b):
    return lax.dot_general(a, b, (((1,), (1,)), ((), ())), preferred_element_type=jnp.float32)


def eye(width):
    return iota((width, width), 0) == iota((width, width), 1)


def as_row(column):
    return jnp.concatenate(
        [
            jnp.sum(jnp.where(eye(LANES), column[i : i + LANES], 0.0), axis=0, keepdims=True)
            for i in range(0, column.shape[0], LANES)
        ],
        axis=1,
    )


def as_column(row):
    return jnp.concatenate(
        [
            jnp.sum(jnp.where(eye(LANES), row[:, i : i + LANES], 0.0), axis=1, keepdims=True)
            for i in range(0, row.shape[1], LANES)
        ],
        axis=0,
    )


def narrow(value):
    return value.astype(jnp.bfloat16).astype(jnp.float32)


def pack_half(half, core, place, rows, label, put):
    cluster, arrival = label // SPAN, label % SPAN
    owner = cluster % OWNERS
    earlier = (iota((ROWS, ROWS), 0) < iota((ROWS, ROWS), 1)).astype(jnp.bfloat16)
    member = iota((OWNERS, ROWS), 0) == owner
    before = jnp.dot(member.astype(jnp.bfloat16), earlier, preferred_element_type=jnp.float32)
    within = jnp.sum(jnp.where(member, before, 0.0), axis=0, keepdims=True).astype(jnp.int32)
    mine = owner % 2 == core
    slot = owner // 2 * CAPACITY + within

    wide = rows[...].astype(jnp.float32)
    norm = as_row(jnp.sum(wide * wide, axis=1, keepdims=True))
    high = narrow(norm)
    middle = narrow(norm - high)
    digits = (cluster + 1, arrival % 256, arrival // 256 % 256, arrival // 65536)
    digits = [digit.astype(jnp.float32) for digit in digits] + [high, middle, norm - high - middle]
    digits = jnp.concatenate(digits + [jnp.zeros((1, ROWS), jnp.float32)], axis=0).astype(jnp.bfloat16)

    lane = iota((8, LANES), 1)
    begin = place * SLOTS + half * CAPACITY
    window = (lane >= begin) & (lane < begin + CAPACITY)
    labels = []
    step = LANES // CAPACITY
    for g in range(0, GROUPS, step):
        pick = (iota((LANES, ROWS), 0) + g * CAPACITY == jnp.where(mine, slot, -1)).astype(jnp.bfloat16)
        moved = jnp.dot(pick, rows[...], preferred_element_type=jnp.float32).astype(jnp.bfloat16)
        moved = moved.reshape(step, CAPACITY, D)
        for k in range(TILES):
            put(g, step, k, moved[:, :, k * LANES : (k + 1) * LANES])
        line = nt(digits, pick)
        for j in range(step):
            turn = (begin + LANES - j * CAPACITY) % LANES
            labels.append(jnp.where(window, pltpu.roll(line, turn, 1), 0.0))
    return jnp.where(mine, slot, slot + HALF), labels


def pack_own_kernel(where_ref, rows_ref, label_ref, half_ref, labels_ref, slot_ref):
    def put(g, step, k, value):
        half_ref[g : g + step, k * CAPACITY : (k + 1) * CAPACITY, :] = value

    slot, labels = pack_half(0, where_ref[0], where_ref[1], rows_ref, label_ref[...], put)
    slot_ref[...] = slot
    for g in range(GROUPS):
        labels_ref[g] = labels[g]


def pack_own(where, rows, label):
    return pl.pallas_call(
        pack_own_kernel,
        out_shape=(
            jax.ShapeDtypeStruct((GROUPS, TILES * CAPACITY, LANES), jnp.bfloat16),
            jax.ShapeDtypeStruct((GROUPS, 8, LANES), jnp.float32),
            jax.ShapeDtypeStruct((1, ROWS), jnp.int32),
        ),
        in_specs=[SMEM] + [VMEM] * 2,
        out_specs=(VMEM,) * 3,
        compiler_params=pltpu.CompilerParams(vmem_limit_bytes=16 * 2**20),
        cost_estimate=pl.CostEstimate(flops=2**30, bytes_accessed=2**21, transcendentals=0),
    )(where, rows, label)


def pack_other_kernel(where_ref, rows_ref, label_ref, half_ref, labels_ref, first_ref, second_ref):
    def place(k, half):
        out_ref, tile = (first_ref, k) if k < PARTS[0] else (second_ref, k - PARTS[0])
        return out_ref, tile * SLOTS + half * CAPACITY

    def put(g, step, k, value):
        out_ref, at = place(k, 1)
        out_ref[g : g + step, at : at + CAPACITY, :] = value

    for k in range(TILES):
        out_ref, at = place(k, 0)
        out_ref[:, at : at + CAPACITY, :] = half_ref[:, k * CAPACITY : (k + 1) * CAPACITY, :]
    _, labels = pack_half(1, where_ref[0], where_ref[1], rows_ref, label_ref[...], put)
    for g in range(GROUPS):
        first_ref[g, LABELS:, :] = (labels[g] + labels_ref[g]).astype(jnp.bfloat16)


def pack_other(where, rows, label, half, labels):
    return pl.pallas_call(
        pack_other_kernel,
        out_shape=tuple(
            jax.ShapeDtypeStruct((GROUPS, height, LANES), jnp.bfloat16) for height in HEIGHTS
        ),
        in_specs=[SMEM] + [VMEM] * 4,
        out_specs=(VMEM,) * 2,
        compiler_params=pltpu.CompilerParams(vmem_limit_bytes=16 * 2**20),
    )(where, rows, label, half, labels)


def info(ref):
    tiles = ref[:, LABELS:, :].astype(jnp.float32).reshape(GROUPS // PER_TILE, PER_TILE, 8, LANES)
    rows = jnp.concatenate([jnp.sum(tiles[t], axis=0) for t in range(GROUPS // PER_TILE)], axis=1)
    cluster = rows[0:1] - 1.0
    arrival = rows[1:2] + 256.0 * rows[2:3] + 65536.0 * rows[3:4]
    inverse = lax.rsqrt(rows[4:5] + rows[5:6] + rows[6:7] + EPSILON)
    return cluster, arrival, inverse


def row_keys(cluster, arrival):
    base = cluster.astype(jnp.int32) * SPAN
    return base, base + arrival.astype(jnp.int32)


def column_keys(cluster, arrival):
    return as_column(cluster).astype(jnp.int32) * SPAN + as_column(arrival).astype(jnp.int32)


def unfold(source, target, count, at=0):
    for k in range(count):
        target[:, (at + k) * LANES : (at + k + 1) * LANES] = source[
            :, k * SLOTS : (k + 1) * SLOTS, :
        ].reshape(PANEL, LANES)


WIDTH = 256
CUTS = [slice(start, start + WIDTH) for start in range(0, PANEL, WIDTH)]


def head_kernel(
    first_ref, below_ref, above_ref, own_below, own_above, below_above, inverse_ref, own, below, above
):
    unfold(first_ref, own, PARTS[0])
    unfold(below_ref, below, PARTS[0])
    unfold(above_ref, above, PARTS[0])
    cluster, arrival, inverse_ref[0:1] = info(first_ref)
    own_base, own_limit = row_keys(cluster, arrival)
    cluster, arrival, inverse_ref[1:2] = info(below_ref)
    below_base, below_limit = row_keys(cluster, arrival)
    below_key = column_keys(cluster, arrival)
    cluster, arrival, inverse_ref[2:3] = info(above_ref)
    above_key = column_keys(cluster, arrival)

    def masked(key, base, limit, scores):
        return jnp.where((key < limit) & (key >= base), scores, NONE)

    for at in CUTS:
        own_below[at, :] = masked(below_key[at], own_base, own_limit, nt(below[at, :], own[...]))
        own_above[at, :] = masked(above_key[at], own_base, own_limit, nt(above[at, :], own[...]))
        below_above[at, :] = masked(above_key[at], below_base, below_limit, nt(above[at, :], below[...]))


def score_head(first, below, above):
    return pl.pallas_call(
        head_kernel,
        out_shape=(SQUARE, SQUARE, SQUARE, jax.ShapeDtypeStruct((8, PANEL), jnp.float32)),
        in_specs=[VMEM] * 3,
        out_specs=(VMEM,) * 4,
        scratch_shapes=[pltpu.VMEM((PANEL, HEAD), jnp.bfloat16)] * 3,
        compiler_params=pltpu.CompilerParams(vmem_limit_bytes=32 * 2**20),
        cost_estimate=pl.CostEstimate(flops=6 * 2**30, bytes_accessed=2**24, transcendentals=0),
    )(first, below, above)


def own_kernel(first_ref, second_ref, best_ref, own):
    unfold(first_ref, own, PARTS[0])
    unfold(second_ref, own, PARTS[1], PARTS[0])
    cluster, arrival, inverse = info(first_ref)
    base, limit = row_keys(cluster, arrival)
    key, scale = column_keys(cluster, arrival), as_column(inverse)
    best = jnp.full((1, PANEL), NONE, jnp.float32)
    for at in CUTS:
        value = nt(own[at, :], own[...]) * scale[at]
        value = jnp.where((key[at] < limit) & (key[at] >= base), value, NONE)
        best = jnp.maximum(best, jnp.max(value, axis=0, keepdims=True))
    best_ref[...] = best


def score_own(first, second):
    return pl.pallas_call(
        own_kernel,
        out_shape=LINE,
        in_specs=[VMEM] * 2,
        out_specs=VMEM,
        scratch_shapes=[pltpu.VMEM((PANEL, D), jnp.bfloat16)],
        compiler_params=pltpu.CompilerParams(vmem_limit_bytes=20 * 2**20),
        cost_estimate=pl.CostEstimate(flops=3 * 2**30, bytes_accessed=2**22, transcendentals=0),
    )(first, second)


def tail_kernel(
    best_ref,
    own_below,
    own_above,
    below_above,
    inverse_ref,
    second_ref,
    below_ref,
    above_ref,
    out_ref,
    own,
    below,
    above,
):
    for source, target in ((second_ref, own), (below_ref, below), (above_ref, above)):
        unfold(source, target, PARTS[1])
    below_scale, above_scale = as_column(inverse_ref[1:2]), as_column(inverse_ref[2:3])
    own_best, below_best = best_ref[...], jnp.full((1, PANEL), NONE, jnp.float32)

    def fold(best, value):
        return jnp.maximum(best, jnp.max(value, axis=0, keepdims=True))

    for at in CUTS:
        value = (own_below[at, :] + nt(below[at, :], own[...])) * below_scale[at]
        own_best = fold(own_best, value)
        value = (own_above[at, :] + nt(above[at, :], own[...])) * above_scale[at]
        own_best = fold(own_best, value)
        value = (below_above[at, :] + nt(above[at, :], below[...])) * above_scale[at]
        below_best = fold(below_best, value)
    own_best = jnp.maximum(own_best * inverse_ref[0:1], -1.0)
    below_best = jnp.maximum(below_best * inverse_ref[1:2], -1.0)

    shape = (PER_TILE, LANES)
    window, turn = iota(shape, 1) // SLOTS, iota(shape, 0)
    for t in range(GROUPS // PER_TILE):
        at = slice(t * LANES, (t + 1) * LANES)
        near = jnp.broadcast_to(own_best[:, at], shape)
        far = jnp.broadcast_to(pltpu.roll(below_best[:, at], LANES // 2, 1), shape)
        out_ref[t * PER_TILE : (t + 1) * PER_TILE, :] = jnp.where(
            window == turn, near, jnp.where(window == (turn + PER_TILE // 2) % PER_TILE, far, -1.0)
        )


def score_tail(best, head, second, below, above):
    return pl.pallas_call(
        tail_kernel,
        out_shape=jax.ShapeDtypeStruct((GROUPS, LANES), jnp.float32),
        in_specs=[VMEM] * 8,
        out_specs=VMEM,
        scratch_shapes=[pltpu.VMEM((PANEL, TAIL), jnp.bfloat16)] * 3,
        compiler_params=pltpu.CompilerParams(vmem_limit_bytes=28 * 2**20),
    )(best, *head, second, below, above)


def unpack_kernel(where_ref, own_ref, own_far_ref, other_ref, other_far_ref, slot_ref, out_ref):
    slot = slot_ref[...]
    half = slot // HALF
    blocks = jnp.concatenate(
        [
            jnp.maximum(near[...], pltpu.roll(far[...], LANES // 2, 1))
            for near, far in ((own_ref, own_far_ref), (other_ref, other_far_ref))
        ],
        axis=0,
    )
    high = narrow(blocks)
    middle = narrow(blocks - high)
    parts = jnp.concatenate([high, middle, blocks - high - middle], axis=1).astype(jnp.bfloat16)
    member = (iota((2 * GROUPS, ROWS), 0) == slot // CAPACITY).astype(jnp.bfloat16)
    every = lax.dot_general(
        parts, member, (((0,), (0,)), ((), ())), preferred_element_type=jnp.float32
    )
    place = jnp.where(half == 0, where_ref[1], where_ref[2])
    lane = place * SLOTS + half * CAPACITY + slot % CAPACITY
    out_ref[...] = jnp.sum(
        jnp.where(iota((3 * LANES, ROWS), 0) % LANES == lane, every, 0.0), axis=0, keepdims=True
    )


def unpack(where, own, own_far, other, other_far, slot):
    return pl.pallas_call(
        unpack_kernel,
        out_shape=jax.ShapeDtypeStruct((1, ROWS), jnp.float32),
        in_specs=[SMEM] + [VMEM] * 5,
        out_specs=VMEM,
        compiler_params=pltpu.CompilerParams(vmem_limit_bytes=4 * 2**20),
    )(where, own, own_far, other, other_far, slot).reshape(ROWS)


def device(z, x, core, y):
    return ((z * X + x) * 2 + core) * Y + y


PLACES = [(z, x, y) for z in range(Z) for x in range(X) for y in range(Y)]
OWNER_GROUPS = [[device(z, x, 0, y) for z in range(Z) for x in range(X)] for y in range(Y)] + [
    [device(z, x, 1, y) for z in range(Z) for y in range(Y)] for x in range(X)
]


def to_owners(array):
    return lax.all_to_all(
        array, AXES, split_axis=0, concat_axis=0, tiled=True, axis_index_groups=OWNER_GROUPS
    )


def passed_along(array, by, cross=0):
    pairs = []
    for z, x, y in PLACES:
        pairs.append((device(z, x, 0, y), device(z, x, cross, (y + by) % Y)))
        pairs.append((device(z, x, 1, y), device(z, (x + by) % X, 1 - cross, y)))
    return lax.ppermute(array, AXES, pairs)


def other_core(array):
    size = lax.axis_size("shard")
    return lax.ppermute(array, "shard", [(i, i ^ 1) for i in range(size)])


def per_device(embeddings, cluster, arrival):
    label = (cluster * SPAN + arrival).reshape(1, ROWS)
    shard, y = lax.axis_index("shard"), lax.axis_index("clus")
    core, x = shard % 2, shard // 2 % X
    where = jnp.stack([core, jnp.where(core == 0, x, y), jnp.where(core == 0, y, x)])
    half, labels, slot = pack_own(where, embeddings, label)
    first, second = pack_other(where, other_core(embeddings), other_core(label), half, labels)
    own_first = to_owners(first)
    below_first, above_first = passed_along(own_first, 1), passed_along(own_first, -1)
    own_second = to_owners(second)
    below_second, above_second = passed_along(own_second, 1), passed_along(own_second, -1)
    head = score_head(own_first, below_first, above_first)
    best = score_own(own_first, own_second)
    block = to_owners(score_tail(best, head, own_second, below_second, above_second))
    near, far, across = other_core(block), passed_along(block, -1), passed_along(block, -1, 1)
    return unpack(where, block, far, near, across, slot)


def solution(mesh):
    in_specs = (P(("shard", "clus"), None), P(("shard", "clus")), P(("shard", "clus")))
    out_specs = P(("shard", "clus"))
    return jax.shard_map(
        per_device, mesh=mesh, in_specs=in_specs, out_specs=out_specs, check_vma=False
    )
```

```python
import jax
import jax.numpy as jnp
from jax import lax
from jax.experimental import pallas as pl
from jax.experimental.pallas import tpu as pltpu
from jax.sharding import PartitionSpec as P

EPSILON = 1e-06
OWNERS = 64
CAPACITY = 16
ROWS = 512
D = 1024
GROUPS = 32
SLOTS = 2 * CAPACITY
PANEL = GROUPS * SLOTS
HALF = GROUPS * CAPACITY
LANES = 128
PER_TILE = LANES // SLOTS
TILES = D // LANES
PARTS = (6, 2)
LABELS = PARTS[0] * SLOTS
HEIGHTS = (LABELS + 8, PARTS[1] * SLOTS)
HEAD = PARTS[0] * LANES
TAIL = PARTS[1] * LANES
SPAN = 131072
NONE = float("-inf")
Z, X, Y = 8, 4, 4
AXES = ("shard", "clus")
VMEM = pl.BlockSpec(memory_space=pltpu.VMEM)
SMEM = pl.BlockSpec(memory_space=pltpu.SMEM)
LINE = jax.ShapeDtypeStruct((1, PANEL), jnp.float32)
SQUARE = jax.ShapeDtypeStruct((PANEL, PANEL), jnp.float32)


def iota(shape, dim):
    return lax.broadcasted_iota(jnp.int32, shape, dim)


def nt(a, b):
    return lax.dot_general(a, b, (((1,), (1,)), ((), ())), preferred_element_type=jnp.float32)


def eye(width):
    return iota((width, width), 0) == iota((width, width), 1)


def as_row(column):
    return jnp.concatenate(
        [
            jnp.sum(jnp.where(eye(LANES), column[i : i + LANES], 0.0), axis=0, keepdims=True)
            for i in range(0, column.shape[0], LANES)
        ],
        axis=1,
    )


def as_column(row):
    return jnp.concatenate(
        [
            jnp.sum(jnp.where(eye(LANES), row[:, i : i + LANES], 0.0), axis=1, keepdims=True)
            for i in range(0, row.shape[1], LANES)
        ],
        axis=0,
    )


def narrow(value):
    return value.astype(jnp.bfloat16).astype(jnp.float32)


def pack_half(half, core, place, rows, label, put):
    cluster, arrival = label // SPAN, label % SPAN
    owner = cluster % OWNERS
    earlier = (iota((ROWS, ROWS), 0) < iota((ROWS, ROWS), 1)).astype(jnp.bfloat16)
    member = iota((OWNERS, ROWS), 0) == owner
    before = jnp.dot(member.astype(jnp.bfloat16), earlier, preferred_element_type=jnp.float32)
    within = jnp.sum(jnp.where(member, before, 0.0), axis=0, keepdims=True).astype(jnp.int32)
    mine = owner % 2 == core
    slot = owner // 2 * CAPACITY + within

    wide = rows[...].astype(jnp.float32)
    norm = as_row(jnp.sum(wide * wide, axis=1, keepdims=True))
    high = narrow(norm)
    middle = narrow(norm - high)
    digits = (cluster + 1, arrival % 256, arrival // 256 % 256, arrival // 65536)
    digits = [digit.astype(jnp.float32) for digit in digits] + [high, middle, norm - high - middle]
    digits = jnp.concatenate(digits + [jnp.zeros((1, ROWS), jnp.float32)], axis=0).astype(jnp.bfloat16)

    lane = iota((8, LANES), 1)
    begin = place * SLOTS + half * CAPACITY
    window = (lane >= begin) & (lane < begin + CAPACITY)
    labels = []
    step = LANES // CAPACITY
    for g in range(0, GROUPS, step):
        pick = (iota((LANES, ROWS), 0) + g * CAPACITY == jnp.where(mine, slot, -1)).astype(jnp.bfloat16)
        moved = jnp.dot(pick, rows[...], preferred_element_type=jnp.float32).astype(jnp.bfloat16)
        moved = moved.reshape(step, CAPACITY, D)
        for k in range(TILES):
            put(g, step, k, moved[:, :, k * LANES : (k + 1) * LANES])
        line = nt(digits, pick)
        for j in range(step):
            turn = (begin + LANES - j * CAPACITY) % LANES
            labels.append(jnp.where(window, pltpu.roll(line, turn, 1), 0.0))
    return jnp.where(mine, slot, slot + HALF), labels


def pack_own_kernel(where_ref, rows_ref, label_ref, half_ref, labels_ref, slot_ref):
    def put(g, step, k, value):
        half_ref[g : g + step, k * CAPACITY : (k + 1) * CAPACITY, :] = value

    slot, labels = pack_half(0, where_ref[0], where_ref[1], rows_ref, label_ref[...], put)
    slot_ref[...] = slot
    for g in range(GROUPS):
        labels_ref[g] = labels[g]


def pack_own(where, rows, label):
    return pl.pallas_call(
        pack_own_kernel,
        out_shape=(
            jax.ShapeDtypeStruct((GROUPS, TILES * CAPACITY, LANES), jnp.bfloat16),
            jax.ShapeDtypeStruct((GROUPS, 8, LANES), jnp.float32),
            jax.ShapeDtypeStruct((1, ROWS), jnp.int32),
        ),
        in_specs=[SMEM] + [VMEM] * 2,
        out_specs=(VMEM,) * 3,
        compiler_params=pltpu.CompilerParams(vmem_limit_bytes=16 * 2**20),
        cost_estimate=pl.CostEstimate(flops=2**30, bytes_accessed=2**21, transcendentals=0),
    )(where, rows, label)


def pack_other_kernel(where_ref, rows_ref, label_ref, half_ref, labels_ref, first_ref, second_ref):
    def place(k, half):
        out_ref, tile = (first_ref, k) if k < PARTS[0] else (second_ref, k - PARTS[0])
        return out_ref, tile * SLOTS + half * CAPACITY

    def put(g, step, k, value):
        out_ref, at = place(k, 1)
        out_ref[g : g + step, at : at + CAPACITY, :] = value

    for k in range(TILES):
        out_ref, at = place(k, 0)
        out_ref[:, at : at + CAPACITY, :] = half_ref[:, k * CAPACITY : (k + 1) * CAPACITY, :]
    _, labels = pack_half(1, where_ref[0], where_ref[1], rows_ref, label_ref[...], put)
    for g in range(GROUPS):
        first_ref[g, LABELS:, :] = (labels[g] + labels_ref[g]).astype(jnp.bfloat16)


def pack_other(where, rows, label, half, labels):
    return pl.pallas_call(
        pack_other_kernel,
        out_shape=tuple(
            jax.ShapeDtypeStruct((GROUPS, height, LANES), jnp.bfloat16) for height in HEIGHTS
        ),
        in_specs=[SMEM] + [VMEM] * 4,
        out_specs=(VMEM,) * 2,
        compiler_params=pltpu.CompilerParams(vmem_limit_bytes=16 * 2**20),
    )(where, rows, label, half, labels)


def info(ref):
    tiles = ref[:, LABELS:, :].astype(jnp.float32).reshape(GROUPS // PER_TILE, PER_TILE, 8, LANES)
    rows = jnp.concatenate([jnp.sum(tiles[t], axis=0) for t in range(GROUPS // PER_TILE)], axis=1)
    cluster = rows[0:1] - 1.0
    arrival = rows[1:2] + 256.0 * rows[2:3] + 65536.0 * rows[3:4]
    inverse = lax.rsqrt(rows[4:5] + rows[5:6] + rows[6:7] + EPSILON)
    return cluster, arrival, inverse


def row_keys(cluster, arrival):
    base = cluster.astype(jnp.int32) * SPAN
    return base, base + arrival.astype(jnp.int32)


def column_keys(cluster, arrival):
    return as_column(cluster).astype(jnp.int32) * SPAN + as_column(arrival).astype(jnp.int32)


def unfold(source, target, count, at=0):
    for k in range(count):
        target[:, (at + k) * LANES : (at + k + 1) * LANES] = source[
            :, k * SLOTS : (k + 1) * SLOTS, :
        ].reshape(PANEL, LANES)


WIDTH = 256
CUTS = [slice(start, start + WIDTH) for start in range(0, PANEL, WIDTH)]


def head_kernel(
    first_ref, below_ref, above_ref, own_below, own_above, below_above, inverse_ref, own, below, above
):
    unfold(first_ref, own, PARTS[0])
    unfold(below_ref, below, PARTS[0])
    unfold(above_ref, above, PARTS[0])
    cluster, arrival, inverse_ref[0:1] = info(first_ref)
    own_base, own_limit = row_keys(cluster, arrival)
    cluster, arrival, inverse_ref[1:2] = info(below_ref)
    below_base, below_limit = row_keys(cluster, arrival)
    below_key = column_keys(cluster, arrival)
    cluster, arrival, inverse_ref[2:3] = info(above_ref)
    above_key = column_keys(cluster, arrival)

    def masked(key, base, limit, scores):
        return jnp.where((key < limit) & (key >= base), scores, NONE)

    for at in CUTS:
        own_below[at, :] = masked(below_key[at], own_base, own_limit, nt(below[at, :], own[...]))
        own_above[at, :] = masked(above_key[at], own_base, own_limit, nt(above[at, :], own[...]))
        below_above[at, :] = masked(above_key[at], below_base, below_limit, nt(above[at, :], below[...]))


def score_head(first, below, above):
    return pl.pallas_call(
        head_kernel,
        out_shape=(SQUARE, SQUARE, SQUARE, jax.ShapeDtypeStruct((8, PANEL), jnp.float32)),
        in_specs=[VMEM] * 3,
        out_specs=(VMEM,) * 4,
        scratch_shapes=[pltpu.VMEM((PANEL, HEAD), jnp.bfloat16)] * 3,
        compiler_params=pltpu.CompilerParams(vmem_limit_bytes=32 * 2**20),
        cost_estimate=pl.CostEstimate(flops=6 * 2**30, bytes_accessed=2**24, transcendentals=0),
    )(first, below, above)


def own_kernel(first_ref, second_ref, best_ref, own):
    unfold(first_ref, own, PARTS[0])
    unfold(second_ref, own, PARTS[1], PARTS[0])
    cluster, arrival, inverse = info(first_ref)
    base, limit = row_keys(cluster, arrival)
    key, scale = column_keys(cluster, arrival), as_column(inverse)
    best = jnp.full((1, PANEL), NONE, jnp.float32)
    for at in CUTS:
        value = nt(own[at, :], own[...]) * scale[at]
        value = jnp.where((key[at] < limit) & (key[at] >= base), value, NONE)
        best = jnp.maximum(best, jnp.max(value, axis=0, keepdims=True))
    best_ref[...] = best


def score_own(first, second):
    return pl.pallas_call(
        own_kernel,
        out_shape=LINE,
        in_specs=[VMEM] * 2,
        out_specs=VMEM,
        scratch_shapes=[pltpu.VMEM((PANEL, D), jnp.bfloat16)],
        compiler_params=pltpu.CompilerParams(vmem_limit_bytes=20 * 2**20),
        cost_estimate=pl.CostEstimate(flops=3 * 2**30, bytes_accessed=2**22, transcendentals=0),
    )(first, second)


def finish(best, inverse):
    line = jnp.maximum(best * inverse, -1.0)
    return jnp.concatenate(
        [
            jnp.broadcast_to(line[:, t * LANES : (t + 1) * LANES], (PER_TILE, LANES))
            for t in range(GROUPS // PER_TILE)
        ],
        axis=0,
    )


def fold(best, head, keys, queries, scale):
    for at in CUTS:
        value = (head[at, :] + nt(keys[at, :], queries[...])) * scale[at]
        best = jnp.maximum(best, jnp.max(value, axis=0, keepdims=True))
    return best


def far_kernel(below_above, inverse_ref, below_ref, above_ref, out_ref, below, above):
    unfold(below_ref, below, PARTS[1])
    unfold(above_ref, above, PARTS[1])
    best = jnp.full((1, PANEL), NONE, jnp.float32)
    best = fold(best, below_above, above, below, as_column(inverse_ref[2:3]))
    out_ref[...] = finish(best, inverse_ref[1:2])


def score_far(below_above, inverse, below, above):
    return pl.pallas_call(
        far_kernel,
        out_shape=jax.ShapeDtypeStruct((GROUPS, LANES), jnp.float32),
        in_specs=[VMEM] * 4,
        out_specs=VMEM,
        scratch_shapes=[pltpu.VMEM((PANEL, TAIL), jnp.bfloat16)] * 2,
        compiler_params=pltpu.CompilerParams(vmem_limit_bytes=16 * 2**20),
        cost_estimate=pl.CostEstimate(flops=2**29, bytes_accessed=2**23, transcendentals=0),
    )(below_above, inverse, below, above)


def near_kernel(
    best_ref,
    own_below,
    own_above,
    inverse_ref,
    second_ref,
    below_ref,
    above_ref,
    out_ref,
    own,
    below,
    above,
):
    for source, target in ((second_ref, own), (below_ref, below), (above_ref, above)):
        unfold(source, target, PARTS[1])
    best = fold(best_ref[...], own_below, below, own, as_column(inverse_ref[1:2]))
    best = fold(best, own_above, above, own, as_column(inverse_ref[2:3]))
    out_ref[...] = finish(best, inverse_ref[0:1])


def score_near(best, own_below, own_above, inverse, second, below, above):
    return pl.pallas_call(
        near_kernel,
        out_shape=jax.ShapeDtypeStruct((GROUPS, LANES), jnp.float32),
        in_specs=[VMEM] * 7,
        out_specs=VMEM,
        scratch_shapes=[pltpu.VMEM((PANEL, TAIL), jnp.bfloat16)] * 3,
        compiler_params=pltpu.CompilerParams(vmem_limit_bytes=24 * 2**20),
        cost_estimate=pl.CostEstimate(flops=2**30, bytes_accessed=2**24, transcendentals=0),
    )(best, own_below, own_above, inverse, second, below, above)


def unpack_kernel(where_ref, own_ref, other_ref, slot_ref, out_ref):
    slot = slot_ref[...]
    half = slot // HALF
    blocks = jnp.concatenate([own_ref[...], other_ref[...]], axis=0)
    high = narrow(blocks)
    middle = narrow(blocks - high)
    parts = jnp.concatenate([high, middle, blocks - high - middle], axis=1).astype(jnp.bfloat16)
    member = (iota((2 * GROUPS, ROWS), 0) == slot // CAPACITY).astype(jnp.bfloat16)
    every = lax.dot_general(
        parts, member, (((0,), (0,)), ((), ())), preferred_element_type=jnp.float32
    )
    place = jnp.where(half == 0, where_ref[1], where_ref[2])
    lane = place * SLOTS + half * CAPACITY + slot % CAPACITY
    out_ref[...] = jnp.sum(
        jnp.where(iota((3 * LANES, ROWS), 0) % LANES == lane, every, 0.0), axis=0, keepdims=True
    )


def unpack(where, own, other, slot):
    return pl.pallas_call(
        unpack_kernel,
        out_shape=jax.ShapeDtypeStruct((1, ROWS), jnp.float32),
        in_specs=[SMEM] + [VMEM] * 3,
        out_specs=VMEM,
        compiler_params=pltpu.CompilerParams(vmem_limit_bytes=4 * 2**20),
    )(where, own, other, slot).reshape(ROWS)


def device(z, x, core, y):
    return ((z * X + x) * 2 + core) * Y + y


PLACES = [(z, x, y) for z in range(Z) for x in range(X) for y in range(Y)]
OWNER_GROUPS = [[device(z, x, 0, y) for z in range(Z) for x in range(X)] for y in range(Y)] + [
    [device(z, x, 1, y) for z in range(Z) for y in range(Y)] for x in range(X)
]


def to_owners(array):
    return lax.all_to_all(
        array, AXES, split_axis=0, concat_axis=0, tiled=True, axis_index_groups=OWNER_GROUPS
    )


def passed_along(array, by):
    pairs = []
    for z, x, y in PLACES:
        pairs.append((device(z, x, 0, y), device(z, x, 0, (y + by) % Y)))
        pairs.append((device(z, x, 1, y), device(z, (x + by) % X, 1, y)))
    return lax.ppermute(array, AXES, pairs)


def other_core(array):
    size = lax.axis_size("shard")
    return lax.ppermute(array, "shard", [(i, i ^ 1) for i in range(size)])


def per_device(embeddings, cluster, arrival):
    label = (cluster * SPAN + arrival).reshape(1, ROWS)
    shard, y = lax.axis_index("shard"), lax.axis_index("clus")
    core, x = shard % 2, shard // 2 % X
    where = jnp.stack([core, jnp.where(core == 0, x, y), jnp.where(core == 0, y, x)])
    half, labels, slot = pack_own(where, embeddings, label)
    first, second = pack_other(where, other_core(embeddings), other_core(label), half, labels)
    own_first = to_owners(first)
    below_first, above_first = passed_along(own_first, 1), passed_along(own_first, -1)
    own_second = to_owners(second)
    below_second, above_second = passed_along(own_second, 1), passed_along(own_second, -1)
    own_below, own_above, below_above, inverse = score_head(own_first, below_first, above_first)
    best = score_own(own_first, own_second)
    far = passed_along(score_far(below_above, inverse, below_second, above_second), -1)
    near = score_near(best, own_below, own_above, inverse, own_second, below_second, above_second)
    block = to_owners(jnp.maximum(near, far))
    return unpack(where, block, other_core(block), slot)


def solution(mesh):
    in_specs = (P(("shard", "clus"), None), P(("shard", "clus")), P(("shard", "clus")))
    out_specs = P(("shard", "clus"))
    return jax.shard_map(
        per_device, mesh=mesh, in_specs=in_specs, out_specs=out_specs, check_vma=False
    )
```

```python
import jax
import jax.numpy as jnp
from jax import lax
from jax.experimental import pallas as pl
from jax.experimental.pallas import tpu as pltpu
from jax.sharding import PartitionSpec as P

EPSILON = 1e-06
OWNERS = 64
CAPACITY = 16
ROWS = 512
D = 1024
GROUPS = 32
SLOTS = 2 * CAPACITY
PANEL = GROUPS * SLOTS
HALF = GROUPS * CAPACITY
LANES = 128
PER_TILE = LANES // SLOTS
TILES = D // LANES
PARTS = (6, 2)
LABELS = PARTS[0] * SLOTS
HEIGHTS = (LABELS + 8, PARTS[1] * SLOTS)
HEAD = PARTS[0] * LANES
TAIL = PARTS[1] * LANES
SPAN = 131072
NONE = float("-inf")
Z, X, Y = 8, 4, 4
AXES = ("shard", "clus")
VMEM = pl.BlockSpec(memory_space=pltpu.VMEM)
LINE = jax.ShapeDtypeStruct((1, PANEL), jnp.float32)
SQUARE = jax.ShapeDtypeStruct((PANEL, PANEL), jnp.float32)


def iota(shape, dim):
    return lax.broadcasted_iota(jnp.int32, shape, dim)


def nt(a, b):
    return lax.dot_general(a, b, (((1,), (1,)), ((), ())), preferred_element_type=jnp.float32)


def eye(width):
    return iota((width, width), 0) == iota((width, width), 1)


def as_row(column):
    return jnp.concatenate(
        [
            jnp.sum(jnp.where(eye(LANES), column[i : i + LANES], 0.0), axis=0, keepdims=True)
            for i in range(0, column.shape[0], LANES)
        ],
        axis=1,
    )


def as_column(row):
    return jnp.concatenate(
        [
            jnp.sum(jnp.where(eye(LANES), row[:, i : i + LANES], 0.0), axis=1, keepdims=True)
            for i in range(0, row.shape[1], LANES)
        ],
        axis=0,
    )


def narrow(value):
    return value.astype(jnp.bfloat16).astype(jnp.float32)


def whereabouts():
    shard, y = lax.axis_index("shard"), lax.axis_index("clus")
    core, x = shard % 2, shard // 2 % X
    return core, jnp.where(core == 0, x, y), jnp.where(core == 0, y, x)


def pack_half(half, rows, label, put):
    core, place, _ = whereabouts()
    cluster, arrival = label // SPAN, label % SPAN
    owner = cluster % OWNERS
    earlier = (iota((ROWS, ROWS), 0) < iota((ROWS, ROWS), 1)).astype(jnp.bfloat16)
    member = iota((OWNERS, ROWS), 0) == owner
    before = jnp.dot(member.astype(jnp.bfloat16), earlier, preferred_element_type=jnp.float32)
    within = jnp.sum(jnp.where(member, before, 0.0), axis=0, keepdims=True).astype(jnp.int32)
    mine = owner % 2 == core
    slot = owner // 2 * CAPACITY + within

    wide = rows[...].astype(jnp.float32)
    norm = as_row(jnp.sum(wide * wide, axis=1, keepdims=True))
    high = narrow(norm)
    middle = narrow(norm - high)
    digits = (cluster + 1, arrival % 256, arrival // 256 % 256, arrival // 65536)
    digits = [digit.astype(jnp.float32) for digit in digits] + [high, middle, norm - high - middle]
    digits = jnp.concatenate(digits + [jnp.zeros((1, ROWS), jnp.float32)], axis=0).astype(jnp.bfloat16)

    lane = iota((8, LANES), 1)
    begin = place * SLOTS + half * CAPACITY
    window = (lane >= begin) & (lane < begin + CAPACITY)
    labels = []
    step = GROUPS
    for g in range(0, GROUPS, step):
        count = step * CAPACITY
        pick = (iota((count, ROWS), 0) + g * CAPACITY == jnp.where(mine, slot, -1)).astype(jnp.bfloat16)
        moved = jnp.dot(pick, rows[...], preferred_element_type=jnp.float32).astype(jnp.bfloat16)
        moved = moved.reshape(step, CAPACITY, D)
        for k in range(TILES):
            put(g, step, k, moved[:, :, k * LANES : (k + 1) * LANES])
        line = nt(digits, pick)
        for j in range(0, count, CAPACITY):
            tile = line[:, j // LANES * LANES : (j // LANES + 1) * LANES]
            turn = (begin + LANES - j % LANES) % LANES
            labels.append(jnp.where(window, pltpu.roll(tile, turn, 1), 0.0))
    return jnp.where(mine, slot, slot + HALF), labels


def pack_own_kernel(rows_ref, label_ref, half_ref, labels_ref, slot_ref):
    def put(g, step, k, value):
        half_ref[g : g + step, k * CAPACITY : (k + 1) * CAPACITY, :] = value

    slot, labels = pack_half(0, rows_ref, label_ref[...], put)
    slot_ref[...] = slot
    for g in range(GROUPS):
        labels_ref[g] = labels[g]


def pack_own(rows, label):
    return pl.pallas_call(
        pack_own_kernel,
        out_shape=(
            jax.ShapeDtypeStruct((GROUPS, TILES * CAPACITY, LANES), jnp.bfloat16),
            jax.ShapeDtypeStruct((GROUPS, 8, LANES), jnp.float32),
            jax.ShapeDtypeStruct((1, ROWS), jnp.int32),
        ),
        in_specs=[VMEM] * 2,
        out_specs=(VMEM,) * 3,
        compiler_params=pltpu.CompilerParams(vmem_limit_bytes=16 * 2**20),
        cost_estimate=pl.CostEstimate(flops=2**30, bytes_accessed=2**21, transcendentals=0),
    )(rows, label)


def pack_other_kernel(rows_ref, label_ref, half_ref, labels_ref, first_ref, second_ref):
    def place(k, half):
        out_ref, tile = (first_ref, k) if k < PARTS[0] else (second_ref, k - PARTS[0])
        return out_ref, tile * SLOTS + half * CAPACITY

    def put(g, step, k, value):
        out_ref, at = place(k, 1)
        out_ref[g : g + step, at : at + CAPACITY, :] = value

    for k in range(TILES):
        out_ref, at = place(k, 0)
        out_ref[:, at : at + CAPACITY, :] = half_ref[:, k * CAPACITY : (k + 1) * CAPACITY, :]
    _, labels = pack_half(1, rows_ref, label_ref[...], put)
    for g in range(GROUPS):
        first_ref[g, LABELS:, :] = (labels[g] + labels_ref[g]).astype(jnp.bfloat16)


def pack_other(rows, label, half, labels):
    return pl.pallas_call(
        pack_other_kernel,
        out_shape=tuple(
            jax.ShapeDtypeStruct((GROUPS, height, LANES), jnp.bfloat16) for height in HEIGHTS
        ),
        in_specs=[VMEM] * 4,
        out_specs=(VMEM,) * 2,
        compiler_params=pltpu.CompilerParams(vmem_limit_bytes=16 * 2**20),
    )(rows, label, half, labels)


def info(ref):
    tiles = ref[:, LABELS:, :].astype(jnp.float32).reshape(GROUPS // PER_TILE, PER_TILE, 8, LANES)
    rows = jnp.concatenate([jnp.sum(tiles[t], axis=0) for t in range(GROUPS // PER_TILE)], axis=1)
    cluster = rows[0:1] - 1.0
    arrival = rows[1:2] + 256.0 * rows[2:3] + 65536.0 * rows[3:4]
    inverse = lax.rsqrt(rows[4:5] + rows[5:6] + rows[6:7] + EPSILON)
    return cluster, arrival, inverse


def row_keys(cluster, arrival):
    base = cluster.astype(jnp.int32) * SPAN
    return base, base + arrival.astype(jnp.int32)


def column_keys(cluster, arrival):
    return as_column(cluster).astype(jnp.int32) * SPAN + as_column(arrival).astype(jnp.int32)


def unfold(source, target, count, at=0):
    for k in range(count):
        target[:, (at + k) * LANES : (at + k + 1) * LANES] = source[
            :, k * SLOTS : (k + 1) * SLOTS, :
        ].reshape(PANEL, LANES)


WIDTH = 512
CUTS = [slice(start, start + WIDTH) for start in range(0, PANEL, WIDTH)]


def head_kernel(
    first_ref, below_ref, above_ref, own_below, own_above, below_above, inverse_ref, own, below, above
):
    unfold(first_ref, own, PARTS[0])
    unfold(below_ref, below, PARTS[0])
    unfold(above_ref, above, PARTS[0])
    cluster, arrival, inverse_ref[0:1] = info(first_ref)
    own_base, own_limit = row_keys(cluster, arrival)
    cluster, arrival, inverse_ref[1:2] = info(below_ref)
    below_base, below_limit = row_keys(cluster, arrival)
    below_key = column_keys(cluster, arrival)
    cluster, arrival, inverse_ref[2:3] = info(above_ref)
    above_key = column_keys(cluster, arrival)

    def masked(key, base, limit, scores):
        return jnp.where((key < limit) & (key >= base), scores, NONE)

    for at in CUTS:
        own_below[at, :] = masked(below_key[at], own_base, own_limit, nt(below[at, :], own[...]))
        own_above[at, :] = masked(above_key[at], own_base, own_limit, nt(above[at, :], own[...]))
        below_above[at, :] = masked(above_key[at], below_base, below_limit, nt(above[at, :], below[...]))


def score_head(first, below, above):
    return pl.pallas_call(
        head_kernel,
        out_shape=(SQUARE, SQUARE, SQUARE, jax.ShapeDtypeStruct((8, PANEL), jnp.float32)),
        in_specs=[VMEM] * 3,
        out_specs=(VMEM,) * 4,
        scratch_shapes=[pltpu.VMEM((PANEL, HEAD), jnp.bfloat16)] * 3,
        compiler_params=pltpu.CompilerParams(vmem_limit_bytes=32 * 2**20),
        cost_estimate=pl.CostEstimate(flops=6 * 2**30, bytes_accessed=2**24, transcendentals=0),
    )(first, below, above)


def own_kernel(first_ref, second_ref, best_ref, own):
    unfold(first_ref, own, PARTS[0])
    unfold(second_ref, own, PARTS[1], PARTS[0])
    cluster, arrival, inverse = info(first_ref)
    base, limit = row_keys(cluster, arrival)
    key, scale = column_keys(cluster, arrival), as_column(inverse)
    best = jnp.full((1, PANEL), NONE, jnp.float32)
    for at in CUTS:
        value = nt(own[at, :], own[...]) * scale[at]
        value = jnp.where((key[at] < limit) & (key[at] >= base), value, NONE)
        best = jnp.maximum(best, jnp.max(value, axis=0, keepdims=True))
    best_ref[...] = best


def score_own(first, second):
    return pl.pallas_call(
        own_kernel,
        out_shape=LINE,
        in_specs=[VMEM] * 2,
        out_specs=VMEM,
        scratch_shapes=[pltpu.VMEM((PANEL, D), jnp.bfloat16)],
        compiler_params=pltpu.CompilerParams(vmem_limit_bytes=20 * 2**20),
        cost_estimate=pl.CostEstimate(flops=3 * 2**30, bytes_accessed=2**22, transcendentals=0),
    )(first, second)


def finish(best, inverse):
    line = jnp.maximum(best * inverse, -1.0)
    return jnp.concatenate(
        [
            jnp.broadcast_to(line[:, t * LANES : (t + 1) * LANES], (PER_TILE, LANES))
            for t in range(GROUPS // PER_TILE)
        ],
        axis=0,
    )


def fold(best, head, keys, queries, scale):
    for at in CUTS:
        value = (head[at, :] + nt(keys[at, :], queries[...])) * scale[at]
        best = jnp.maximum(best, jnp.max(value, axis=0, keepdims=True))
    return best


def far_kernel(below_above, inverse_ref, below_ref, above_ref, out_ref, below, above):
    unfold(below_ref, below, PARTS[1])
    unfold(above_ref, above, PARTS[1])
    best = jnp.full((1, PANEL), NONE, jnp.float32)
    best = fold(best, below_above, above, below, as_column(inverse_ref[2:3]))
    out_ref[...] = finish(best, inverse_ref[1:2])


def score_far(below_above, inverse, below, above):
    return pl.pallas_call(
        far_kernel,
        out_shape=jax.ShapeDtypeStruct((GROUPS, LANES), jnp.float32),
        in_specs=[VMEM] * 4,
        out_specs=VMEM,
        scratch_shapes=[pltpu.VMEM((PANEL, TAIL), jnp.bfloat16)] * 2,
        compiler_params=pltpu.CompilerParams(vmem_limit_bytes=16 * 2**20),
        cost_estimate=pl.CostEstimate(flops=2**29, bytes_accessed=2**23, transcendentals=0),
    )(below_above, inverse, below, above)


def near_kernel(
    best_ref,
    own_below,
    own_above,
    inverse_ref,
    second_ref,
    below_ref,
    above_ref,
    out_ref,
    own,
    below,
    above,
):
    for source, target in ((second_ref, own), (below_ref, below), (above_ref, above)):
        unfold(source, target, PARTS[1])
    best = fold(best_ref[...], own_below, below, own, as_column(inverse_ref[1:2]))
    best = fold(best, own_above, above, own, as_column(inverse_ref[2:3]))
    out_ref[...] = finish(best, inverse_ref[0:1])


def score_near(best, own_below, own_above, inverse, second, below, above):
    return pl.pallas_call(
        near_kernel,
        out_shape=jax.ShapeDtypeStruct((GROUPS, LANES), jnp.float32),
        in_specs=[VMEM] * 7,
        out_specs=VMEM,
        scratch_shapes=[pltpu.VMEM((PANEL, TAIL), jnp.bfloat16)] * 3,
        compiler_params=pltpu.CompilerParams(vmem_limit_bytes=24 * 2**20),
        cost_estimate=pl.CostEstimate(flops=2**30, bytes_accessed=2**24, transcendentals=0),
    )(best, own_below, own_above, inverse, second, below, above)


def unpack_kernel(own_ref, other_ref, slot_ref, out_ref):
    slot = slot_ref[...]
    half = slot // HALF
    blocks = jnp.concatenate([own_ref[...], other_ref[...]], axis=0)
    high = narrow(blocks)
    middle = narrow(blocks - high)
    parts = jnp.concatenate([high, middle, blocks - high - middle], axis=1).astype(jnp.bfloat16)
    member = (iota((2 * GROUPS, ROWS), 0) == slot // CAPACITY).astype(jnp.bfloat16)
    every = lax.dot_general(
        parts, member, (((0,), (0,)), ((), ())), preferred_element_type=jnp.float32
    )
    _, place, other_place = whereabouts()
    place = jnp.where(half == 0, place, other_place)
    lane = place * SLOTS + half * CAPACITY + slot % CAPACITY
    out_ref[...] = jnp.sum(
        jnp.where(iota((3 * LANES, ROWS), 0) % LANES == lane, every, 0.0), axis=0, keepdims=True
    )


def unpack(own, other, slot):
    return pl.pallas_call(
        unpack_kernel,
        out_shape=jax.ShapeDtypeStruct((1, ROWS), jnp.float32),
        in_specs=[VMEM] * 3,
        out_specs=VMEM,
        compiler_params=pltpu.CompilerParams(vmem_limit_bytes=4 * 2**20),
    )(own, other, slot).reshape(ROWS)


def device(z, x, core, y):
    return ((z * X + x) * 2 + core) * Y + y


PLACES = [(z, x, y) for z in range(Z) for x in range(X) for y in range(Y)]
OWNER_GROUPS = [[device(z, x, 0, y) for z in range(Z) for x in range(X)] for y in range(Y)] + [
    [device(z, x, 1, y) for z in range(Z) for y in range(Y)] for x in range(X)
]


def to_owners(array):
    return lax.all_to_all(
        array, AXES, split_axis=0, concat_axis=0, tiled=True, axis_index_groups=OWNER_GROUPS
    )


def passed_along(array, by):
    pairs = []
    for z, x, y in PLACES:
        pairs.append((device(z, x, 0, y), device(z, x, 0, (y + by) % Y)))
        pairs.append((device(z, x, 1, y), device(z, (x + by) % X, 1, y)))
    return lax.ppermute(array, AXES, pairs)


def other_core(array):
    size = lax.axis_size("shard")
    return lax.ppermute(array, "shard", [(i, i ^ 1) for i in range(size)])


def per_device(embeddings, cluster, arrival):
    label = (cluster * SPAN + arrival).reshape(1, ROWS)
    half, labels, slot = pack_own(embeddings, label)
    first, second = pack_other(other_core(embeddings), other_core(label), half, labels)
    own_first = to_owners(first)
    below_first, above_first = passed_along(own_first, 1), passed_along(own_first, -1)
    own_second = to_owners(second)
    below_second, above_second = passed_along(own_second, 1), passed_along(own_second, -1)
    own_below, own_above, below_above, inverse = score_head(own_first, below_first, above_first)
    best = score_own(own_first, own_second)
    far = passed_along(score_far(below_above, inverse, below_second, above_second), -1)
    near = score_near(best, own_below, own_above, inverse, own_second, below_second, above_second)
    block = to_owners(jnp.maximum(near, far))
    return unpack(block, other_core(block), slot)


def solution(mesh):
    in_specs = (P(("shard", "clus"), None), P(("shard", "clus")), P(("shard", "clus")))
    out_specs = P(("shard", "clus"))
    return jax.shard_map(
        per_device, mesh=mesh, in_specs=in_specs, out_specs=out_specs, check_vma=False
    )
```

```python
import jax
import jax.numpy as jnp
from jax import lax
from jax.experimental import pallas as pl
from jax.experimental.pallas import tpu as pltpu
from jax.sharding import PartitionSpec as P

EPSILON = 1e-06
OWNERS = 64
CAPACITY = 16
ROWS = 512
D = 1024
GROUPS = 32
SLOTS = 2 * CAPACITY
PANEL = GROUPS * SLOTS
HALF = GROUPS * CAPACITY
LANES = 128
PER_TILE = LANES // SLOTS
TILES = D // LANES
PARTS = (6, 2)
LABELS = PARTS[0] * SLOTS
HEIGHTS = (LABELS + 8, PARTS[1] * SLOTS)
HEAD = PARTS[0] * LANES
TAIL = PARTS[1] * LANES
SPAN = 131072
NONE = float("-inf")
Z, X, Y = 8, 4, 4
AXES = ("shard", "clus")
FIRST = (5, 2)
VMEM = pl.BlockSpec(memory_space=pltpu.VMEM)
LINE = jax.ShapeDtypeStruct((1, PANEL), jnp.float32)
SQUARE = jax.ShapeDtypeStruct((PANEL, PANEL), jnp.float32)


def iota(shape, dim):
    return lax.broadcasted_iota(jnp.int32, shape, dim)


def nt(a, b):
    return lax.dot_general(a, b, (((1,), (1,)), ((), ())), preferred_element_type=jnp.float32)


def eye(width):
    return iota((width, width), 0) == iota((width, width), 1)


def as_row(column):
    return jnp.concatenate(
        [
            jnp.sum(jnp.where(eye(LANES), column[i : i + LANES], 0.0), axis=0, keepdims=True)
            for i in range(0, column.shape[0], LANES)
        ],
        axis=1,
    )


def as_column(row):
    return jnp.concatenate(
        [
            jnp.sum(jnp.where(eye(LANES), row[:, i : i + LANES], 0.0), axis=1, keepdims=True)
            for i in range(0, row.shape[1], LANES)
        ],
        axis=0,
    )


def narrow(value):
    return value.astype(jnp.bfloat16).astype(jnp.float32)


def whereabouts():
    shard, y = lax.axis_index("shard"), lax.axis_index("clus")
    core, x = shard % 2, shard // 2 % X
    x, y = ((i + PER_TILE - FIRST[1]) % PER_TILE for i in (x, y))
    return core, jnp.where(core == 0, x, y), jnp.where(core == 0, y, x)


def pack_half(half, rows, cluster, arrival, put, wait=lambda: None):
    core, place, _ = whereabouts()
    owner = cluster % OWNERS
    earlier = (iota((ROWS, ROWS), 0) < iota((ROWS, ROWS), 1)).astype(jnp.bfloat16)
    member = iota((OWNERS, ROWS), 0) == owner
    before = jnp.dot(member.astype(jnp.bfloat16), earlier, preferred_element_type=jnp.float32)
    within = jnp.sum(jnp.where(member, before, 0.0), axis=0, keepdims=True).astype(jnp.int32)
    mine = owner % 2 == core
    slot = owner // 2 * CAPACITY + within

    wait()
    wide = rows[...].astype(jnp.float32)
    norm = as_row(jnp.sum(wide * wide, axis=1, keepdims=True))
    high = narrow(norm)
    middle = narrow(norm - high)
    digits = (cluster + 1, arrival % 256, arrival // 256 % 256, arrival // 65536)
    digits = [digit.astype(jnp.float32) for digit in digits] + [high, middle, norm - high - middle]
    digits = jnp.concatenate(digits + [jnp.zeros((1, ROWS), jnp.float32)], axis=0).astype(jnp.bfloat16)

    lane = iota((8, LANES), 1)
    begin = place * SLOTS + half * CAPACITY
    window = (lane >= begin) & (lane < begin + CAPACITY)
    labels = []
    step = GROUPS
    for g in range(0, GROUPS, step):
        count = step * CAPACITY
        pick = (iota((count, ROWS), 0) + g * CAPACITY == jnp.where(mine, slot, -1)).astype(jnp.bfloat16)
        moved = jnp.dot(pick, rows[...], preferred_element_type=jnp.float32).astype(jnp.bfloat16)
        moved = moved.reshape(step, CAPACITY, D)
        for k in range(TILES):
            put(g, step, k, moved[:, :, k * LANES : (k + 1) * LANES])
        line = nt(digits, pick)
        for j in range(0, count, CAPACITY):
            tile = line[:, j // LANES * LANES : (j // LANES + 1) * LANES]
            turn = (begin + LANES - j % LANES) % LANES
            labels.append(jnp.where(window, pltpu.roll(tile, turn, 1), 0.0))
    return jnp.where(mine, slot, slot + HALF), labels


def pack_own_kernel(
    rows_ref, cluster_ref, arrival_ref, half_ref, labels_ref, slot_ref, rows, cluster, arrival, done
):
    def put(g, step, k, value):
        half_ref[g : g + step, k * CAPACITY : (k + 1) * CAPACITY, :] = value

    pairs = ((cluster_ref, cluster), (arrival_ref, arrival), (rows_ref, rows))
    copies = [pltpu.make_async_copy(a, b, done.at[i]) for i, (a, b) in enumerate(pairs)]
    for copy in copies:
        copy.start()
    copies[0].wait()
    copies[1].wait()
    slot, labels = pack_half(0, rows, cluster[...], arrival[...], put, copies[2].wait)
    slot_ref[...] = slot
    for g in range(GROUPS):
        labels_ref[g] = labels[g]


def pack_own(*arrays):
    arrays = [pltpu.with_memory_space_constraint(array, pltpu.HBM) for array in arrays]
    return pl.pallas_call(
        pack_own_kernel,
        out_shape=(
            jax.ShapeDtypeStruct((GROUPS, TILES * CAPACITY, LANES), jnp.bfloat16),
            jax.ShapeDtypeStruct((GROUPS, 8, LANES), jnp.float32),
            jax.ShapeDtypeStruct((1, ROWS), jnp.int32),
        ),
        in_specs=[pl.BlockSpec(memory_space=pltpu.HBM)] * 3,
        out_specs=(VMEM,) * 3,
        scratch_shapes=[
            pltpu.VMEM((ROWS, D), jnp.bfloat16),
            pltpu.VMEM((1, ROWS), jnp.int32),
            pltpu.VMEM((1, ROWS), jnp.int32),
            pltpu.SemaphoreType.DMA((3,)),
        ],
        compiler_params=pltpu.CompilerParams(vmem_limit_bytes=16 * 2**20),
        cost_estimate=pl.CostEstimate(flops=2**30, bytes_accessed=2**21, transcendentals=0),
    )(*arrays)


def pack_other_kernel(
    rows_ref, cluster_ref, arrival_ref, half_ref, labels_ref, first_ref, second_ref
):
    def place(k, half):
        out_ref, tile = (first_ref, k) if k < PARTS[0] else (second_ref, k - PARTS[0])
        return out_ref, tile * SLOTS + half * CAPACITY

    def put(g, step, k, value):
        out_ref, at = place(k, 1)
        out_ref[g : g + step, at : at + CAPACITY, :] = value

    for k in range(TILES):
        out_ref, at = place(k, 0)
        out_ref[:, at : at + CAPACITY, :] = half_ref[:, k * CAPACITY : (k + 1) * CAPACITY, :]
    _, labels = pack_half(1, rows_ref, cluster_ref[...], arrival_ref[...], put)
    for g in range(GROUPS):
        first_ref[g, LABELS:, :] = (labels[g] + labels_ref[g]).astype(jnp.bfloat16)


def pack_other(rows, cluster, arrival, half, labels):
    return pl.pallas_call(
        pack_other_kernel,
        out_shape=tuple(
            jax.ShapeDtypeStruct((GROUPS, height, LANES), jnp.bfloat16) for height in HEIGHTS
        ),
        in_specs=[VMEM] * 5,
        out_specs=(VMEM,) * 2,
        compiler_params=pltpu.CompilerParams(vmem_limit_bytes=16 * 2**20),
    )(rows, cluster, arrival, half, labels)


def info(ref):
    tiles = ref[:, LABELS:, :].astype(jnp.float32).reshape(GROUPS // PER_TILE, PER_TILE, 8, LANES)
    rows = jnp.concatenate([jnp.sum(tiles[t], axis=0) for t in range(GROUPS // PER_TILE)], axis=1)
    cluster = rows[0:1] - 1.0
    arrival = rows[1:2] + 256.0 * rows[2:3] + 65536.0 * rows[3:4]
    inverse = lax.rsqrt(rows[4:5] + rows[5:6] + rows[6:7] + EPSILON)
    return cluster, arrival, inverse


def row_keys(cluster, arrival):
    base = cluster.astype(jnp.int32) * SPAN
    return base, base + arrival.astype(jnp.int32)


def column_keys(cluster, arrival):
    return as_column(cluster).astype(jnp.int32) * SPAN + as_column(arrival).astype(jnp.int32)


def unfold(source, target, count, at=0):
    for k in range(count):
        target[:, (at + k) * LANES : (at + k + 1) * LANES] = source[
            :, k * SLOTS : (k + 1) * SLOTS, :
        ].reshape(PANEL, LANES)


WIDTH = 512
CUTS = [slice(start, start + WIDTH) for start in range(0, PANEL, WIDTH)]


def head_kernel(
    first_ref, below_ref, above_ref, own_below, own_above, below_above, inverse_ref, own, below, above
):
    unfold(first_ref, own, PARTS[0])
    unfold(below_ref, below, PARTS[0])
    unfold(above_ref, above, PARTS[0])
    cluster, arrival, inverse_ref[0:1] = info(first_ref)
    own_base, own_limit = row_keys(cluster, arrival)
    cluster, arrival, inverse_ref[1:2] = info(below_ref)
    below_base, below_limit = row_keys(cluster, arrival)
    below_key = column_keys(cluster, arrival)
    cluster, arrival, inverse_ref[2:3] = info(above_ref)
    above_key = column_keys(cluster, arrival)

    def masked(key, base, limit, scores):
        return jnp.where((key < limit) & (key >= base), scores, NONE)

    for at in CUTS:
        own_below[at, :] = masked(below_key[at], own_base, own_limit, nt(below[at, :], own[...]))
        own_above[at, :] = masked(above_key[at], own_base, own_limit, nt(above[at, :], own[...]))
        below_above[at, :] = masked(above_key[at], below_base, below_limit, nt(above[at, :], below[...]))


def score_head(first, below, above):
    return pl.pallas_call(
        head_kernel,
        out_shape=(SQUARE, SQUARE, SQUARE, jax.ShapeDtypeStruct((8, PANEL), jnp.float32)),
        in_specs=[VMEM] * 3,
        out_specs=(VMEM,) * 4,
        scratch_shapes=[pltpu.VMEM((PANEL, HEAD), jnp.bfloat16)] * 3,
        compiler_params=pltpu.CompilerParams(vmem_limit_bytes=32 * 2**20),
        cost_estimate=pl.CostEstimate(flops=6 * 2**30, bytes_accessed=2**24, transcendentals=0),
    )(first, below, above)


def own_kernel(first_ref, second_ref, best_ref, own):
    unfold(first_ref, own, PARTS[0])
    unfold(second_ref, own, PARTS[1], PARTS[0])
    cluster, arrival, inverse = info(first_ref)
    base, limit = row_keys(cluster, arrival)
    key, scale = column_keys(cluster, arrival), as_column(inverse)
    best = jnp.full((1, PANEL), NONE, jnp.float32)
    for at in CUTS:
        value = nt(own[at, :], own[...]) * scale[at]
        value = jnp.where((key[at] < limit) & (key[at] >= base), value, NONE)
        best = jnp.maximum(best, jnp.max(value, axis=0, keepdims=True))
    best_ref[...] = best


def score_own(first, second):
    return pl.pallas_call(
        own_kernel,
        out_shape=LINE,
        in_specs=[VMEM] * 2,
        out_specs=VMEM,
        scratch_shapes=[pltpu.VMEM((PANEL, D), jnp.bfloat16)],
        compiler_params=pltpu.CompilerParams(vmem_limit_bytes=20 * 2**20),
        cost_estimate=pl.CostEstimate(flops=3 * 2**30, bytes_accessed=2**22, transcendentals=0),
    )(first, second)


def finish(best, inverse):
    line = jnp.maximum(best * inverse, -1.0)
    return jnp.concatenate(
        [
            jnp.broadcast_to(line[:, t * LANES : (t + 1) * LANES], (PER_TILE, LANES))
            for t in range(GROUPS // PER_TILE)
        ],
        axis=0,
    )


def fold(best, head, keys, queries, scale):
    for at in CUTS:
        value = (head[at, :] + nt(keys[at, :], queries[...])) * scale[at]
        best = jnp.maximum(best, jnp.max(value, axis=0, keepdims=True))
    return best


def far_kernel(below_above, inverse_ref, below_ref, above_ref, out_ref, below, above):
    unfold(below_ref, below, PARTS[1])
    unfold(above_ref, above, PARTS[1])
    best = jnp.full((1, PANEL), NONE, jnp.float32)
    best = fold(best, below_above, above, below, as_column(inverse_ref[2:3]))
    out_ref[...] = finish(best, inverse_ref[1:2])


def score_far(below_above, inverse, below, above):
    return pl.pallas_call(
        far_kernel,
        out_shape=jax.ShapeDtypeStruct((GROUPS, LANES), jnp.float32),
        in_specs=[VMEM] * 4,
        out_specs=VMEM,
        scratch_shapes=[pltpu.VMEM((PANEL, TAIL), jnp.bfloat16)] * 2,
        compiler_params=pltpu.CompilerParams(vmem_limit_bytes=16 * 2**20),
        cost_estimate=pl.CostEstimate(flops=2**29, bytes_accessed=2**23, transcendentals=0),
    )(below_above, inverse, below, above)


def near_kernel(
    best_ref,
    own_below,
    own_above,
    inverse_ref,
    second_ref,
    below_ref,
    above_ref,
    out_ref,
    own,
    below,
    above,
):
    for source, target in ((second_ref, own), (below_ref, below), (above_ref, above)):
        unfold(source, target, PARTS[1])
    best = fold(best_ref[...], own_below, below, own, as_column(inverse_ref[1:2]))
    best = fold(best, own_above, above, own, as_column(inverse_ref[2:3]))
    out_ref[...] = finish(best, inverse_ref[0:1])


def score_near(best, own_below, own_above, inverse, second, below, above):
    return pl.pallas_call(
        near_kernel,
        out_shape=jax.ShapeDtypeStruct((GROUPS, LANES), jnp.float32),
        in_specs=[VMEM] * 7,
        out_specs=VMEM,
        scratch_shapes=[pltpu.VMEM((PANEL, TAIL), jnp.bfloat16)] * 3,
        compiler_params=pltpu.CompilerParams(vmem_limit_bytes=24 * 2**20),
        cost_estimate=pl.CostEstimate(flops=2**30, bytes_accessed=2**24, transcendentals=0),
    )(best, own_below, own_above, inverse, second, below, above)


def unpack_kernel(own_ref, other_ref, slot_ref, out_ref):
    slot = slot_ref[...]
    half = slot // HALF
    blocks = jnp.concatenate([own_ref[...], other_ref[...]], axis=0)
    high = narrow(blocks)
    middle = narrow(blocks - high)
    parts = jnp.concatenate([high, middle, blocks - high - middle], axis=1).astype(jnp.bfloat16)
    member = (iota((2 * GROUPS, ROWS), 0) == slot // CAPACITY).astype(jnp.bfloat16)
    every = lax.dot_general(
        parts, member, (((0,), (0,)), ((), ())), preferred_element_type=jnp.float32
    )
    _, place, other_place = whereabouts()
    place = jnp.where(half == 0, place, other_place)
    lane = place * SLOTS + half * CAPACITY + slot % CAPACITY
    out_ref[...] = jnp.sum(
        jnp.where(iota((3 * LANES, ROWS), 0) % LANES == lane, every, 0.0), axis=0, keepdims=True
    )


def unpack(own, other, slot):
    return pl.pallas_call(
        unpack_kernel,
        out_shape=jax.ShapeDtypeStruct((1, ROWS), jnp.float32),
        in_specs=[VMEM] * 3,
        out_specs=VMEM,
        compiler_params=pltpu.CompilerParams(vmem_limit_bytes=4 * 2**20),
    )(own, other, slot).reshape(ROWS)


def device(z, x, core, y):
    return ((z * X + x) * 2 + core) * Y + y


PLACES = [(z, x, y) for z in range(Z) for x in range(X) for y in range(Y)]
ORDER = [(z + FIRST[0]) % Z for z in range(Z)]
TURN = [(i + FIRST[1]) % PER_TILE for i in range(PER_TILE)]
OWNER_GROUPS = [[device(z, x, 0, y) for z in ORDER for x in TURN] for y in range(Y)] + [
    [device(z, x, 1, y) for z in ORDER for y in TURN] for x in range(X)
]


def to_owners(array):
    return lax.all_to_all(
        array, AXES, split_axis=0, concat_axis=0, tiled=True, axis_index_groups=OWNER_GROUPS
    )


def passed_along(array, by):
    pairs = []
    for z, x, y in PLACES:
        pairs.append((device(z, x, 0, y), device(z, x, 0, (y + by) % Y)))
        pairs.append((device(z, x, 1, y), device(z, (x + by) % X, 1, y)))
    return lax.ppermute(array, AXES, pairs)


def other_core(array):
    size = lax.axis_size("shard")
    return lax.ppermute(array, "shard", [(i, i ^ 1) for i in range(size)])


def per_device(embeddings, cluster, arrival):
    arrays = (embeddings, cluster.reshape(1, ROWS), arrival.reshape(1, ROWS))
    half, labels, slot = pack_own(*arrays)
    first, second = pack_other(*[other_core(array) for array in arrays], half, labels)
    own_first = to_owners(first)
    below_first, above_first = passed_along(own_first, 1), passed_along(own_first, -1)
    own_second = to_owners(second)
    below_second, above_second = passed_along(own_second, 1), passed_along(own_second, -1)
    own_below, own_above, below_above, inverse = score_head(own_first, below_first, above_first)
    best = score_own(own_first, own_second)
    far = passed_along(score_far(below_above, inverse, below_second, above_second), -1)
    near = score_near(best, own_below, own_above, inverse, own_second, below_second, above_second)
    block = to_owners(jnp.maximum(near, far))
    return unpack(block, other_core(block), slot)


def solution(mesh):
    in_specs = (P(("shard", "clus"), None), P(("shard", "clus")), P(("shard", "clus")))
    out_specs = P(("shard", "clus"))
    return jax.shard_map(
        per_device, mesh=mesh, in_specs=in_specs, out_specs=out_specs, check_vma=False
    )
```

```python
import jax
import jax.numpy as jnp
from jax import lax
from jax.experimental import pallas as pl
from jax.experimental.pallas import tpu as pltpu
from jax.sharding import PartitionSpec as P

EPSILON = 1e-06
OWNERS = 64
CAPACITY = 16
ROWS = 512
D = 1024
GROUPS = 32
SLOTS = 2 * CAPACITY
PANEL = GROUPS * SLOTS
HALF = GROUPS * CAPACITY
LANES = 128
PER_TILE = LANES // SLOTS
TILES = D // LANES
PARTS = (6, 2)
LABELS = PARTS[0] * SLOTS
HEIGHTS = (LABELS + 8, PARTS[1] * SLOTS)
HEAD = PARTS[0] * LANES
TAIL = PARTS[1] * LANES
SPAN = 131072
NONE = float("-inf")
Z, X, Y = 8, 4, 4
AXES = ("shard", "clus")
FIRST = (5, 2)
VMEM = pl.BlockSpec(memory_space=pltpu.VMEM)
LINE = jax.ShapeDtypeStruct((1, PANEL), jnp.float32)
SQUARE = jax.ShapeDtypeStruct((PANEL, PANEL), jnp.float32)


def iota(shape, dim):
    return lax.broadcasted_iota(jnp.int32, shape, dim)


def nt(a, b):
    return lax.dot_general(a, b, (((1,), (1,)), ((), ())), preferred_element_type=jnp.float32)


def eye(width):
    return iota((width, width), 0) == iota((width, width), 1)


def as_row(column):
    return jnp.concatenate(
        [
            jnp.sum(jnp.where(eye(LANES), column[i : i + LANES], 0.0), axis=0, keepdims=True)
            for i in range(0, column.shape[0], LANES)
        ],
        axis=1,
    )


def as_column(row):
    return jnp.concatenate(
        [
            jnp.sum(jnp.where(eye(LANES), row[:, i : i + LANES], 0.0), axis=1, keepdims=True)
            for i in range(0, row.shape[1], LANES)
        ],
        axis=0,
    )


def narrow(value):
    return value.astype(jnp.bfloat16).astype(jnp.float32)


def whereabouts():
    shard, y = lax.axis_index("shard"), lax.axis_index("clus")
    core, x = shard % 2, shard // 2 % X
    x, y = ((i + PER_TILE - FIRST[1]) % PER_TILE for i in (x, y))
    return core, jnp.where(core == 0, x, y), jnp.where(core == 0, y, x)


def pack_half(half, rows, cluster, arrival, put, wait=lambda: None):
    core, place, _ = whereabouts()
    owner = cluster % OWNERS
    earlier = (iota((ROWS, ROWS), 0) < iota((ROWS, ROWS), 1)).astype(jnp.bfloat16)
    member = iota((OWNERS, ROWS), 0) == owner
    before = jnp.dot(member.astype(jnp.bfloat16), earlier, preferred_element_type=jnp.float32)
    within = jnp.sum(jnp.where(member, before, 0.0), axis=0, keepdims=True).astype(jnp.int32)
    mine = owner % 2 == core
    slot = owner // 2 * CAPACITY + within

    wait()
    wide = rows[...].astype(jnp.float32)
    norm = as_row(jnp.sum(wide * wide, axis=1, keepdims=True))
    high = narrow(norm)
    middle = narrow(norm - high)
    digits = (cluster + 1, arrival % 256, arrival // 256 % 256, arrival // 65536)
    digits = [digit.astype(jnp.float32) for digit in digits] + [high, middle, norm - high - middle]
    digits = jnp.concatenate(digits + [jnp.zeros((1, ROWS), jnp.float32)], axis=0).astype(jnp.bfloat16)

    lane = iota((8, LANES), 1)
    begin = place * SLOTS + half * CAPACITY
    window = (lane >= begin) & (lane < begin + CAPACITY)
    labels = []
    step = GROUPS
    for g in range(0, GROUPS, step):
        count = step * CAPACITY
        pick = (iota((count, ROWS), 0) + g * CAPACITY == jnp.where(mine, slot, -1)).astype(jnp.bfloat16)
        moved = jnp.dot(pick, rows[...], preferred_element_type=jnp.float32).astype(jnp.bfloat16)
        moved = moved.reshape(step, CAPACITY, D)
        for k in range(TILES):
            put(g, step, k, moved[:, :, k * LANES : (k + 1) * LANES])
        line = nt(digits, pick)
        for j in range(0, count, CAPACITY):
            tile = line[:, j // LANES * LANES : (j // LANES + 1) * LANES]
            turn = (begin + LANES - j % LANES) % LANES
            labels.append(jnp.where(window, pltpu.roll(tile, turn, 1), 0.0))
    return jnp.where(mine, slot, slot + HALF), labels


def pack_own_kernel(
    rows_ref, cluster_ref, arrival_ref, half_ref, labels_ref, slot_ref, rows, cluster, arrival, done
):
    def put(g, step, k, value):
        half_ref[g : g + step, k * CAPACITY : (k + 1) * CAPACITY, :] = value

    pairs = ((cluster_ref, cluster), (arrival_ref, arrival), (rows_ref, rows))
    copies = [pltpu.make_async_copy(a, b, done.at[i]) for i, (a, b) in enumerate(pairs)]
    for copy in copies:
        copy.start()
    copies[0].wait()
    copies[1].wait()
    slot, labels = pack_half(0, rows, cluster[...], arrival[...], put, copies[2].wait)
    slot_ref[...] = slot
    for g in range(GROUPS):
        labels_ref[g] = labels[g]


def pack_own(*arrays):
    arrays = [pltpu.with_memory_space_constraint(array, pltpu.HBM) for array in arrays]
    return pl.pallas_call(
        pack_own_kernel,
        out_shape=(
            jax.ShapeDtypeStruct((GROUPS, TILES * CAPACITY, LANES), jnp.bfloat16),
            jax.ShapeDtypeStruct((GROUPS, 8, LANES), jnp.float32),
            jax.ShapeDtypeStruct((1, ROWS), jnp.int32),
        ),
        in_specs=[pl.BlockSpec(memory_space=pltpu.HBM)] * 3,
        out_specs=(VMEM,) * 3,
        scratch_shapes=[
            pltpu.VMEM((ROWS, D), jnp.bfloat16),
            pltpu.VMEM((1, ROWS), jnp.int32),
            pltpu.VMEM((1, ROWS), jnp.int32),
            pltpu.SemaphoreType.DMA((3,)),
        ],
        compiler_params=pltpu.CompilerParams(vmem_limit_bytes=16 * 2**20),
        cost_estimate=pl.CostEstimate(flops=2**30, bytes_accessed=2**21, transcendentals=0),
    )(*arrays)


def pack_other_kernel(
    rows_ref, cluster_ref, arrival_ref, half_ref, labels_ref, first_ref, second_ref
):
    def place(k, half):
        out_ref, tile = (first_ref, k) if k < PARTS[0] else (second_ref, k - PARTS[0])
        return out_ref, tile * SLOTS + half * CAPACITY

    def put(g, step, k, value):
        out_ref, at = place(k, 1)
        out_ref[g : g + step, at : at + CAPACITY, :] = value

    for k in range(TILES):
        out_ref, at = place(k, 0)
        out_ref[:, at : at + CAPACITY, :] = half_ref[:, k * CAPACITY : (k + 1) * CAPACITY, :]
    _, labels = pack_half(1, rows_ref, cluster_ref[...], arrival_ref[...], put)
    for g in range(GROUPS):
        first_ref[g, LABELS:, :] = (labels[g] + labels_ref[g]).astype(jnp.bfloat16)


def pack_other(rows, cluster, arrival, half, labels):
    return pl.pallas_call(
        pack_other_kernel,
        out_shape=tuple(
            jax.ShapeDtypeStruct((GROUPS, height, LANES), jnp.bfloat16) for height in HEIGHTS
        ),
        in_specs=[VMEM] * 5,
        out_specs=(VMEM,) * 2,
        compiler_params=pltpu.CompilerParams(vmem_limit_bytes=16 * 2**20),
    )(rows, cluster, arrival, half, labels)


def info(ref):
    tiles = ref[:, LABELS:, :].astype(jnp.float32).reshape(GROUPS // PER_TILE, PER_TILE, 8, LANES)
    rows = jnp.concatenate([jnp.sum(tiles[t], axis=0) for t in range(GROUPS // PER_TILE)], axis=1)
    cluster = rows[0:1] - 1.0
    arrival = rows[1:2] + 256.0 * rows[2:3] + 65536.0 * rows[3:4]
    inverse = lax.rsqrt(rows[4:5] + rows[5:6] + rows[6:7] + EPSILON)
    return cluster, arrival, inverse


def row_keys(cluster, arrival):
    base = cluster.astype(jnp.int32) * SPAN
    return base, base + arrival.astype(jnp.int32)


def column_keys(cluster, arrival):
    return as_column(cluster).astype(jnp.int32) * SPAN + as_column(arrival).astype(jnp.int32)


def unfold(source, target, count, at=0):
    for k in range(count):
        target[:, (at + k) * LANES : (at + k + 1) * LANES] = source[
            :, k * SLOTS : (k + 1) * SLOTS, :
        ].reshape(PANEL, LANES)


WIDTH = 512
CUTS = [slice(start, start + WIDTH) for start in range(0, PANEL, WIDTH)]


def head_kernel(
    first_ref,
    below_ref,
    above_ref,
    own_below,
    own_above,
    below_above,
    inverse_ref,
    below_scale,
    above_scale,
    own,
    below,
    above,
):
    unfold(first_ref, own, PARTS[0])
    unfold(below_ref, below, PARTS[0])
    unfold(above_ref, above, PARTS[0])
    cluster, arrival, inverse_ref[0:1] = info(first_ref)
    own_base, own_limit = row_keys(cluster, arrival)
    cluster, arrival, inverse_ref[1:2] = info(below_ref)
    below_base, below_limit = row_keys(cluster, arrival)
    below_key = column_keys(cluster, arrival)
    cluster, arrival, inverse_ref[2:3] = info(above_ref)
    above_key = column_keys(cluster, arrival)
    below_scale[...] = as_column(inverse_ref[1:2])
    above_scale[...] = as_column(inverse_ref[2:3])

    def masked(key, base, limit, scores):
        return jnp.where((key < limit) & (key >= base), scores, NONE)

    for at in CUTS:
        own_below[at, :] = masked(below_key[at], own_base, own_limit, nt(below[at, :], own[...]))
        own_above[at, :] = masked(above_key[at], own_base, own_limit, nt(above[at, :], own[...]))
        below_above[at, :] = masked(above_key[at], below_base, below_limit, nt(above[at, :], below[...]))


def score_head(first, below, above):
    return pl.pallas_call(
        head_kernel,
        out_shape=(SQUARE, SQUARE, SQUARE, jax.ShapeDtypeStruct((8, PANEL), jnp.float32))
        + (jax.ShapeDtypeStruct((PANEL, 1), jnp.float32),) * 2,
        in_specs=[VMEM] * 3,
        out_specs=(VMEM,) * 6,
        scratch_shapes=[pltpu.VMEM((PANEL, HEAD), jnp.bfloat16)] * 3,
        compiler_params=pltpu.CompilerParams(vmem_limit_bytes=32 * 2**20),
        cost_estimate=pl.CostEstimate(flops=6 * 2**30, bytes_accessed=2**24, transcendentals=0),
    )(first, below, above)


def own_kernel(first_ref, second_ref, best_ref, own):
    unfold(first_ref, own, PARTS[0])
    unfold(second_ref, own, PARTS[1], PARTS[0])
    cluster, arrival, inverse = info(first_ref)
    base, limit = row_keys(cluster, arrival)
    key, scale = column_keys(cluster, arrival), as_column(inverse)
    best = jnp.full((1, PANEL), NONE, jnp.float32)
    for at in CUTS:
        value = nt(own[at, :], own[...]) * scale[at]
        value = jnp.where((key[at] < limit) & (key[at] >= base), value, NONE)
        best = jnp.maximum(best, jnp.max(value, axis=0, keepdims=True))
    best_ref[...] = best


def score_own(first, second):
    return pl.pallas_call(
        own_kernel,
        out_shape=LINE,
        in_specs=[VMEM] * 2,
        out_specs=VMEM,
        scratch_shapes=[pltpu.VMEM((PANEL, D), jnp.bfloat16)],
        compiler_params=pltpu.CompilerParams(vmem_limit_bytes=20 * 2**20),
        cost_estimate=pl.CostEstimate(flops=3 * 2**30, bytes_accessed=2**22, transcendentals=0),
    )(first, second)


def finish(best, inverse):
    line = jnp.maximum(best * inverse, -1.0)
    return jnp.concatenate(
        [
            jnp.broadcast_to(line[:, t * LANES : (t + 1) * LANES], (PER_TILE, LANES))
            for t in range(GROUPS // PER_TILE)
        ],
        axis=0,
    )


def fold(best, head, keys, queries, scale):
    for at in CUTS:
        value = (head[at, :] + nt(keys[at, :], queries[...])) * scale[at]
        best = jnp.maximum(best, jnp.max(value, axis=0, keepdims=True))
    return best


def far_kernel(below_above, inverse_ref, scale, below_ref, above_ref, out_ref, below, above):
    unfold(below_ref, below, PARTS[1])
    unfold(above_ref, above, PARTS[1])
    best = jnp.full((1, PANEL), NONE, jnp.float32)
    best = fold(best, below_above, above, below, scale)
    out_ref[...] = finish(best, inverse_ref[1:2])


def score_far(below_above, inverse, scale, below, above):
    return pl.pallas_call(
        far_kernel,
        out_shape=jax.ShapeDtypeStruct((GROUPS, LANES), jnp.float32),
        in_specs=[VMEM] * 5,
        out_specs=VMEM,
        scratch_shapes=[pltpu.VMEM((PANEL, TAIL), jnp.bfloat16)] * 2,
        compiler_params=pltpu.CompilerParams(vmem_limit_bytes=16 * 2**20),
        cost_estimate=pl.CostEstimate(flops=2**29, bytes_accessed=2**23, transcendentals=0),
    )(below_above, inverse, scale, below, above)


def near_kernel(
    best_ref,
    own_below,
    own_above,
    inverse_ref,
    below_scale,
    above_scale,
    second_ref,
    below_ref,
    above_ref,
    out_ref,
    own,
    below,
    above,
):
    for source, target in ((second_ref, own), (below_ref, below), (above_ref, above)):
        unfold(source, target, PARTS[1])
    best = fold(best_ref[...], own_below, below, own, below_scale)
    best = fold(best, own_above, above, own, above_scale)
    out_ref[...] = finish(best, inverse_ref[0:1])


def score_near(best, own_below, own_above, inverse, scales, second, below, above):
    return pl.pallas_call(
        near_kernel,
        out_shape=jax.ShapeDtypeStruct((GROUPS, LANES), jnp.float32),
        in_specs=[VMEM] * 9,
        out_specs=VMEM,
        scratch_shapes=[pltpu.VMEM((PANEL, TAIL), jnp.bfloat16)] * 3,
        compiler_params=pltpu.CompilerParams(vmem_limit_bytes=24 * 2**20),
        cost_estimate=pl.CostEstimate(flops=2**30, bytes_accessed=2**24, transcendentals=0),
    )(best, own_below, own_above, inverse, *scales, second, below, above)


def unpack_kernel(own_ref, other_ref, slot_ref, out_ref):
    slot = slot_ref[...]
    half = slot // HALF
    blocks = jnp.concatenate([own_ref[...], other_ref[...]], axis=0)
    high = narrow(blocks)
    middle = narrow(blocks - high)
    parts = jnp.concatenate([high, middle, blocks - high - middle], axis=1).astype(jnp.bfloat16)
    member = (iota((2 * GROUPS, ROWS), 0) == slot // CAPACITY).astype(jnp.bfloat16)
    every = lax.dot_general(
        parts, member, (((0,), (0,)), ((), ())), preferred_element_type=jnp.float32
    )
    _, place, other_place = whereabouts()
    place = jnp.where(half == 0, place, other_place)
    lane = place * SLOTS + half * CAPACITY + slot % CAPACITY
    out_ref[...] = jnp.sum(
        jnp.where(iota((3 * LANES, ROWS), 0) % LANES == lane, every, 0.0), axis=0, keepdims=True
    )


def unpack(own, other, slot):
    return pl.pallas_call(
        unpack_kernel,
        out_shape=jax.ShapeDtypeStruct((1, ROWS), jnp.float32),
        in_specs=[VMEM] * 3,
        out_specs=VMEM,
        compiler_params=pltpu.CompilerParams(vmem_limit_bytes=4 * 2**20),
    )(own, other, slot).reshape(ROWS)


def device(z, x, core, y):
    return ((z * X + x) * 2 + core) * Y + y


PLACES = [(z, x, y) for z in range(Z) for x in range(X) for y in range(Y)]
ORDER = [(z + FIRST[0]) % Z for z in range(Z)]
TURN = [(i + FIRST[1]) % PER_TILE for i in range(PER_TILE)]
OWNER_GROUPS = [[device(z, x, 0, y) for z in ORDER for x in TURN] for y in range(Y)] + [
    [device(z, x, 1, y) for z in ORDER for y in TURN] for x in range(X)
]


def to_owners(array):
    return lax.all_to_all(
        array, AXES, split_axis=0, concat_axis=0, tiled=True, axis_index_groups=OWNER_GROUPS
    )


def passed_along(array, by):
    pairs = []
    for z, x, y in PLACES:
        pairs.append((device(z, x, 0, y), device(z, x, 0, (y + by) % Y)))
        pairs.append((device(z, x, 1, y), device(z, (x + by) % X, 1, y)))
    return lax.ppermute(array, AXES, pairs)


def other_core(array):
    size = lax.axis_size("shard")
    return lax.ppermute(array, "shard", [(i, i ^ 1) for i in range(size)])


def per_device(embeddings, cluster, arrival):
    arrays = (embeddings, cluster.reshape(1, ROWS), arrival.reshape(1, ROWS))
    half, labels, slot = pack_own(*arrays)
    first, second = pack_other(*[other_core(array) for array in arrays], half, labels)
    own_first = to_owners(first)
    below_first, above_first = passed_along(own_first, 1), passed_along(own_first, -1)
    own_second = to_owners(second)
    below_second, above_second = passed_along(own_second, 1), passed_along(own_second, -1)
    own_below, own_above, below_above, inverse, *scales = score_head(own_first, below_first, above_first)
    best = score_own(own_first, own_second)
    far = passed_along(score_far(below_above, inverse, scales[1], below_second, above_second), -1)
    near = score_near(
        best, own_below, own_above, inverse, scales, own_second, below_second, above_second
    )
    block = to_owners(jnp.maximum(near, far))
    return unpack(block, other_core(block), slot)


def solution(mesh):
    in_specs = (P(("shard", "clus"), None), P(("shard", "clus")), P(("shard", "clus")))
    out_specs = P(("shard", "clus"))
    return jax.shard_map(
        per_device, mesh=mesh, in_specs=in_specs, out_specs=out_specs, check_vma=False
    )
```

```python
import jax
import jax.numpy as jnp
from jax import lax
from jax.experimental import pallas as pl
from jax.experimental.pallas import tpu as pltpu
from jax.sharding import PartitionSpec as P

EPSILON = 1e-06
OWNERS = 64
CAPACITY = 16
ROWS = 512
D = 1024
GROUPS = 32
SLOTS = 2 * CAPACITY
PANEL = GROUPS * SLOTS
HALF = GROUPS * CAPACITY
LANES = 128
PER_TILE = LANES // SLOTS
TILES = D // LANES
PARTS = (6, 2)
LABELS = PARTS[0] * SLOTS
HEIGHTS = (LABELS + 8, PARTS[1] * SLOTS)
HEAD = PARTS[0] * LANES
TAIL = PARTS[1] * LANES
SPAN = 131072
NONE = float("-inf")
Z, X, Y = 8, 4, 4
AXES = ("shard", "clus")
FIRST = (5, 2)
VMEM = pl.BlockSpec(memory_space=pltpu.VMEM)
LINE = jax.ShapeDtypeStruct((1, PANEL), jnp.float32)
SQUARE = jax.ShapeDtypeStruct((PANEL, PANEL), jnp.float32)


def iota(shape, dim):
    return lax.broadcasted_iota(jnp.int32, shape, dim)


def nt(a, b):
    return lax.dot_general(a, b, (((1,), (1,)), ((), ())), preferred_element_type=jnp.float32)


def eye(width):
    return iota((width, width), 0) == iota((width, width), 1)


def as_row(column):
    return jnp.concatenate(
        [
            jnp.sum(jnp.where(eye(LANES), column[i : i + LANES], 0.0), axis=0, keepdims=True)
            for i in range(0, column.shape[0], LANES)
        ],
        axis=1,
    )


def as_column(row):
    return jnp.concatenate(
        [
            jnp.sum(jnp.where(eye(LANES), row[:, i : i + LANES], 0.0), axis=1, keepdims=True)
            for i in range(0, row.shape[1], LANES)
        ],
        axis=0,
    )


def narrow(value):
    return value.astype(jnp.bfloat16).astype(jnp.float32)


def whereabouts():
    shard, y = lax.axis_index("shard"), lax.axis_index("clus")
    core, x = shard % 2, shard // 2 % X
    x, y = ((i + PER_TILE - FIRST[1]) % PER_TILE for i in (x, y))
    return core, jnp.where(core == 0, x, y), jnp.where(core == 0, y, x)


def pack_half(half, rows, cluster, arrival, put, wait=lambda: None):
    core, place, _ = whereabouts()
    owner = cluster % OWNERS
    earlier = (iota((ROWS, ROWS), 0) < iota((ROWS, ROWS), 1)).astype(jnp.bfloat16)
    member = iota((OWNERS, ROWS), 0) == owner
    before = jnp.dot(member.astype(jnp.bfloat16), earlier, preferred_element_type=jnp.float32)
    within = jnp.sum(jnp.where(member, before, 0.0), axis=0, keepdims=True).astype(jnp.int32)
    mine = owner % 2 == core
    slot = owner // 2 * CAPACITY + within

    wait()
    wide = rows[...].astype(jnp.float32)
    norm = as_row(jnp.sum(wide * wide, axis=1, keepdims=True))
    high = narrow(norm)
    middle = narrow(norm - high)
    digits = (cluster + 1, arrival % 256, arrival // 256 % 256, arrival // 65536)
    digits = [digit.astype(jnp.float32) for digit in digits] + [high, middle, norm - high - middle]
    digits = jnp.concatenate(digits + [jnp.zeros((1, ROWS), jnp.float32)], axis=0).astype(jnp.bfloat16)

    lane = iota((8, LANES), 1)
    begin = place * SLOTS + half * CAPACITY
    window = (lane >= begin) & (lane < begin + CAPACITY)
    labels = []
    step = GROUPS
    for g in range(0, GROUPS, step):
        count = step * CAPACITY
        pick = (iota((count, ROWS), 0) + g * CAPACITY == jnp.where(mine, slot, -1)).astype(jnp.bfloat16)
        moved = jnp.dot(pick, rows[...], preferred_element_type=jnp.float32).astype(jnp.bfloat16)
        moved = moved.reshape(step, CAPACITY, D)
        for k in range(TILES):
            put(g, step, k, moved[:, :, k * LANES : (k + 1) * LANES])
        line = nt(digits, pick)
        for j in range(0, count, CAPACITY):
            tile = line[:, j // LANES * LANES : (j // LANES + 1) * LANES]
            turn = (begin + LANES - j % LANES) % LANES
            labels.append(jnp.where(window, pltpu.roll(tile, turn, 1), 0.0))
    return jnp.where(mine, slot, slot + HALF), labels


def pack_own_kernel(
    rows_ref, cluster_ref, arrival_ref, half_ref, labels_ref, slot_ref, rows, cluster, arrival, done
):
    def put(g, step, k, value):
        half_ref[g : g + step, k * CAPACITY : (k + 1) * CAPACITY, :] = value

    pairs = ((cluster_ref, cluster), (arrival_ref, arrival), (rows_ref, rows))
    copies = [pltpu.make_async_copy(a, b, done.at[i]) for i, (a, b) in enumerate(pairs)]
    for copy in copies:
        copy.start()
    copies[0].wait()
    copies[1].wait()
    slot, labels = pack_half(0, rows, cluster[...], arrival[...], put, copies[2].wait)
    slot_ref[...] = slot
    for g in range(GROUPS):
        labels_ref[g] = labels[g]


def pack_own(*arrays):
    arrays = [pltpu.with_memory_space_constraint(array, pltpu.HBM) for array in arrays]
    return pl.pallas_call(
        pack_own_kernel,
        out_shape=(
            jax.ShapeDtypeStruct((GROUPS, TILES * CAPACITY, LANES), jnp.bfloat16),
            jax.ShapeDtypeStruct((GROUPS, 8, LANES), jnp.float32),
            jax.ShapeDtypeStruct((1, ROWS), jnp.int32),
        ),
        in_specs=[pl.BlockSpec(memory_space=pltpu.HBM)] * 3,
        out_specs=(VMEM,) * 3,
        scratch_shapes=[
            pltpu.VMEM((ROWS, D), jnp.bfloat16),
            pltpu.VMEM((1, ROWS), jnp.int32),
            pltpu.VMEM((1, ROWS), jnp.int32),
            pltpu.SemaphoreType.DMA((3,)),
        ],
        compiler_params=pltpu.CompilerParams(vmem_limit_bytes=16 * 2**20),
        cost_estimate=pl.CostEstimate(flops=2**30, bytes_accessed=2**21, transcendentals=0),
    )(*arrays)


def pack_other_kernel(
    rows_ref, cluster_ref, arrival_ref, half_ref, labels_ref, first_ref, second_ref
):
    def place(k, half):
        out_ref, tile = (first_ref, k) if k < PARTS[0] else (second_ref, k - PARTS[0])
        return out_ref, tile * SLOTS + half * CAPACITY

    def put(g, step, k, value):
        out_ref, at = place(k, 1)
        out_ref[g : g + step, at : at + CAPACITY, :] = value

    for k in range(TILES):
        out_ref, at = place(k, 0)
        out_ref[:, at : at + CAPACITY, :] = half_ref[:, k * CAPACITY : (k + 1) * CAPACITY, :]
    _, labels = pack_half(1, rows_ref, cluster_ref[...], arrival_ref[...], put)
    for g in range(GROUPS):
        first_ref[g, LABELS:, :] = (labels[g] + labels_ref[g]).astype(jnp.bfloat16)


def pack_other(rows, cluster, arrival, half, labels):
    return pl.pallas_call(
        pack_other_kernel,
        out_shape=tuple(
            jax.ShapeDtypeStruct((GROUPS, height, LANES), jnp.bfloat16) for height in HEIGHTS
        ),
        in_specs=[VMEM] * 5,
        out_specs=(VMEM,) * 2,
        compiler_params=pltpu.CompilerParams(vmem_limit_bytes=16 * 2**20),
    )(rows, cluster, arrival, half, labels)


def info(ref):
    tiles = ref[:, LABELS:, :].astype(jnp.float32).reshape(GROUPS // PER_TILE, PER_TILE, 8, LANES)
    rows = jnp.concatenate([jnp.sum(tiles[t], axis=0) for t in range(GROUPS // PER_TILE)], axis=1)
    cluster = rows[0:1] - 1.0
    arrival = rows[1:2] + 256.0 * rows[2:3] + 65536.0 * rows[3:4]
    inverse = lax.rsqrt(rows[4:5] + rows[5:6] + rows[6:7] + EPSILON)
    return cluster, arrival, inverse


def row_keys(cluster, arrival):
    base = cluster.astype(jnp.int32) * SPAN
    return base, base + arrival.astype(jnp.int32)


def column_keys(cluster, arrival):
    return as_column(cluster).astype(jnp.int32) * SPAN + as_column(arrival).astype(jnp.int32)


def unfold(source, target, count, at=0):
    for k in range(count):
        target[:, (at + k) * LANES : (at + k + 1) * LANES] = source[
            :, k * SLOTS : (k + 1) * SLOTS, :
        ].reshape(PANEL, LANES)


WIDTH = 512
CUTS = [slice(start, start + WIDTH) for start in range(0, PANEL, WIDTH)]


def head_kernel(
    first_ref, below_ref, above_ref, own_below, own_above, below_above, inverse_ref, own, below, above
):
    unfold(first_ref, own, PARTS[0])
    unfold(below_ref, below, PARTS[0])
    unfold(above_ref, above, PARTS[0])
    cluster, arrival, inverse_ref[0:1] = info(first_ref)
    own_base, own_limit = row_keys(cluster, arrival)
    cluster, arrival, inverse_ref[1:2] = info(below_ref)
    below_base, below_limit = row_keys(cluster, arrival)
    below_key = column_keys(cluster, arrival)
    cluster, arrival, inverse_ref[2:3] = info(above_ref)
    above_key = column_keys(cluster, arrival)

    def masked(key, base, limit, scores):
        return jnp.where((key < limit) & (key >= base), scores, NONE)

    for at in CUTS:
        own_below[at, :] = masked(below_key[at], own_base, own_limit, nt(below[at, :], own[...]))
        own_above[at, :] = masked(above_key[at], own_base, own_limit, nt(above[at, :], own[...]))
        below_above[at, :] = masked(above_key[at], below_base, below_limit, nt(above[at, :], below[...]))


def score_head(first, below, above):
    return pl.pallas_call(
        head_kernel,
        out_shape=(SQUARE, SQUARE, SQUARE, jax.ShapeDtypeStruct((8, PANEL), jnp.float32)),
        in_specs=[VMEM] * 3,
        out_specs=(VMEM,) * 4,
        scratch_shapes=[pltpu.VMEM((PANEL, HEAD), jnp.bfloat16)] * 3,
        compiler_params=pltpu.CompilerParams(vmem_limit_bytes=32 * 2**20),
        cost_estimate=pl.CostEstimate(flops=6 * 2**30, bytes_accessed=2**24, transcendentals=0),
    )(first, below, above)


def own_kernel(first_ref, second_ref, best_ref, own):
    unfold(first_ref, own, PARTS[0])
    unfold(second_ref, own, PARTS[1], PARTS[0])
    cluster, arrival, inverse = info(first_ref)
    base, limit = row_keys(cluster, arrival)
    key, scale = column_keys(cluster, arrival), as_column(inverse)
    best = jnp.full((1, PANEL), NONE, jnp.float32)
    for at in CUTS:
        value = nt(own[at, :], own[...]) * scale[at]
        value = jnp.where((key[at] < limit) & (key[at] >= base), value, NONE)
        best = jnp.maximum(best, jnp.max(value, axis=0, keepdims=True))
    best_ref[...] = best


def score_own(first, second):
    return pl.pallas_call(
        own_kernel,
        out_shape=LINE,
        in_specs=[VMEM] * 2,
        out_specs=VMEM,
        scratch_shapes=[pltpu.VMEM((PANEL, D), jnp.bfloat16)],
        compiler_params=pltpu.CompilerParams(vmem_limit_bytes=20 * 2**20),
        cost_estimate=pl.CostEstimate(flops=3 * 2**30, bytes_accessed=2**22, transcendentals=0),
    )(first, second)


def finish(best, inverse):
    line = jnp.maximum(best * inverse, -1.0)
    return jnp.concatenate(
        [
            jnp.broadcast_to(line[:, t * LANES : (t + 1) * LANES], (PER_TILE, LANES))
            for t in range(GROUPS // PER_TILE)
        ],
        axis=0,
    )


def fold(best, head, keys, queries, scale):
    for at in CUTS:
        value = (head[at, :] + nt(keys[at, :], queries[...])) * scale[at]
        best = jnp.maximum(best, jnp.max(value, axis=0, keepdims=True))
    return best


def far_kernel(below_above, inverse_ref, below_ref, above_ref, out_ref, below, above):
    unfold(below_ref, below, PARTS[1])
    unfold(above_ref, above, PARTS[1])
    best = jnp.full((1, PANEL), NONE, jnp.float32)
    best = fold(best, below_above, above, below, as_column(inverse_ref[2:3]))
    out_ref[...] = finish(best, inverse_ref[1:2])


def score_far(below_above, inverse, below, above):
    return pl.pallas_call(
        far_kernel,
        out_shape=jax.ShapeDtypeStruct((GROUPS, LANES), jnp.float32),
        in_specs=[VMEM] * 4,
        out_specs=VMEM,
        scratch_shapes=[pltpu.VMEM((PANEL, TAIL), jnp.bfloat16)] * 2,
        compiler_params=pltpu.CompilerParams(vmem_limit_bytes=16 * 2**20),
        cost_estimate=pl.CostEstimate(flops=2**29, bytes_accessed=2**23, transcendentals=0),
    )(below_above, inverse, below, above)


def near_kernel(
    best_ref,
    own_below,
    own_above,
    inverse_ref,
    second_ref,
    below_ref,
    above_ref,
    out_ref,
    own,
    below,
    above,
):
    for source, target in ((second_ref, own), (below_ref, below), (above_ref, above)):
        unfold(source, target, PARTS[1])
    best = fold(best_ref[...], own_below, below, own, as_column(inverse_ref[1:2]))
    best = fold(best, own_above, above, own, as_column(inverse_ref[2:3]))
    out_ref[...] = finish(best, inverse_ref[0:1])


def score_near(best, own_below, own_above, inverse, second, below, above):
    return pl.pallas_call(
        near_kernel,
        out_shape=jax.ShapeDtypeStruct((GROUPS, LANES), jnp.float32),
        in_specs=[VMEM] * 7,
        out_specs=VMEM,
        scratch_shapes=[pltpu.VMEM((PANEL, TAIL), jnp.bfloat16)] * 3,
        compiler_params=pltpu.CompilerParams(vmem_limit_bytes=24 * 2**20),
        cost_estimate=pl.CostEstimate(flops=2**30, bytes_accessed=2**24, transcendentals=0),
    )(best, own_below, own_above, inverse, second, below, above)


def unpack_kernel(own_ref, other_ref, slot_ref, out_ref):
    slot = slot_ref[...]
    half = slot // HALF
    blocks = jnp.concatenate([own_ref[...], other_ref[...]], axis=0)
    high = narrow(blocks)
    middle = narrow(blocks - high)
    parts = jnp.concatenate([high, middle, blocks - high - middle], axis=1).astype(jnp.bfloat16)
    member = (iota((2 * GROUPS, ROWS), 0) == slot // CAPACITY).astype(jnp.bfloat16)
    every = lax.dot_general(
        parts, member, (((0,), (0,)), ((), ())), preferred_element_type=jnp.float32
    )
    _, place, other_place = whereabouts()
    place = jnp.where(half == 0, place, other_place)
    lane = place * SLOTS + half * CAPACITY + slot % CAPACITY
    out_ref[...] = jnp.sum(
        jnp.where(iota((3 * LANES, ROWS), 0) % LANES == lane, every, 0.0), axis=0, keepdims=True
    )


def unpack(own, other, slot):
    return pl.pallas_call(
        unpack_kernel,
        out_shape=jax.ShapeDtypeStruct((1, ROWS), jnp.float32),
        in_specs=[VMEM] * 3,
        out_specs=VMEM,
        compiler_params=pltpu.CompilerParams(vmem_limit_bytes=4 * 2**20),
    )(own, other, slot).reshape(ROWS)


def device(z, x, core, y):
    return ((z * X + x) * 2 + core) * Y + y


PLACES = [(z, x, y) for z in range(Z) for x in range(X) for y in range(Y)]
ORDER = [5,4,3,2,1,0,7,6]
TURN = [(i + FIRST[1]) % PER_TILE for i in range(PER_TILE)]
OWNER_GROUPS = [[device(z, x, 0, y) for z in ORDER for x in TURN] for y in range(Y)] + [
    [device(z, x, 1, y) for z in ORDER for y in TURN] for x in range(X)
]


def to_owners(array):
    return lax.all_to_all(
        array, AXES, split_axis=0, concat_axis=0, tiled=True, axis_index_groups=OWNER_GROUPS
    )


def passed_along(array, by):
    pairs = []
    for z, x, y in PLACES:
        pairs.append((device(z, x, 0, y), device(z, x, 0, (y + by) % Y)))
        pairs.append((device(z, x, 1, y), device(z, (x + by) % X, 1, y)))
    return lax.ppermute(array, AXES, pairs)


def other_core(array):
    size = lax.axis_size("shard")
    return lax.ppermute(array, "shard", [(i, i ^ 1) for i in range(size)])


def per_device(embeddings, cluster, arrival):
    arrays = (embeddings, cluster.reshape(1, ROWS), arrival.reshape(1, ROWS))
    half, labels, slot = pack_own(*arrays)
    first, second = pack_other(*[other_core(array) for array in arrays], half, labels)
    own_first = to_owners(first)
    below_first, above_first = passed_along(own_first, 1), passed_along(own_first, -1)
    own_second = to_owners(second)
    below_second, above_second = passed_along(own_second, 1), passed_along(own_second, -1)
    own_below, own_above, below_above, inverse = score_head(own_first, below_first, above_first)
    best = score_own(own_first, own_second)
    far = passed_along(score_far(below_above, inverse, below_second, above_second), -1)
    near = score_near(best, own_below, own_above, inverse, own_second, below_second, above_second)
    block = to_owners(jnp.maximum(near, far))
    return unpack(block, other_core(block), slot)


def solution(mesh):
    in_specs = (P(("shard", "clus"), None), P(("shard", "clus")), P(("shard", "clus")))
    out_specs = P(("shard", "clus"))
    return jax.shard_map(
        per_device, mesh=mesh, in_specs=in_specs, out_specs=out_specs, check_vma=False
    )
```
